32 devices in a mesh: rep: 2 (over y), tp: 4 (over z), dp: 4 (over x, core).
Axes of the slice: x: 2, y: 2, z: 4, core: 2. Of those that a mesh axis runs over, the one named last changes fastest.
Arguments:
- upstream: bfloat16 [8, 1024, 8192], P(('rep', 'dp'), 'tp'), parts along dimension 0, may hold values from -6 to 6
- hidden: bfloat16 [8, 1024, 16384], P(('rep', 'dp'), None, 'tp'), parts along dimension 0, may hold values from -6 to 6
- frozen_weight: bfloat16 [16384, 8192], P('tp'), may hold values from -0.0625 to 0.0625
- adapter_down_factor: bfloat16 [32, 16, 16384], P('rep', None, 'tp'), parts along dimension 0, may hold values from -0.119628906 to 0.119628906
- adapter_up_factor: bfloat16 [32, 16, 8192], P('rep', None, 'tp'), parts along dimension 0, may hold values from -0.119628906 to 0.119628906
- live_row_counts: int32 [8, 16], P(('rep', 'dp')), parts along dimension 0, may hold values from 0 to 1024, as said below
- adapter_of_block: int32 [8, 8], P(('rep', 'dp')), parts along dimension 0, may hold values from 0 to 15, as said below
- gradient_owner_group: int32 [32], P('rep'), parts along dimension 0, may hold values from 0 to 3, as said below
Outputs:
- grad_hidden: bfloat16 [8, 1024, 16384], P(('rep', 'dp'), None, 'tp'), parts along dimension 0
- grad_down: float32 [32, 16, 16384], P(('rep', 'dp'), None, 'tp'), parts along dimension 0
- grad_up: float32 [32, 16, 8192], P(('rep', 'dp'), None, 'tp'), parts along dimension 0
The draws below stay inside these ranges and needn't reach their ends.
There are 2 independent parts, one for each index of `rep`. The reference program is written for one: setup_inputs(seed, part) draws one part's arguments, and reference() takes and returns one part's arrays. A program takes and returns all parts, laid end to end along the dimension named above; an argument that names none is the same for every part. Nothing has to cross between parts.
Inputs may be any that keep to these rules, and one draw needn't show every extreme that they name: `live_row_counts`: in each group an adapter's rows fill its blocks: with n of its blocks, its count lies from (n - 1) * 128 + 1 to n * 128, and it is 0 with no blocks. `adapter_of_block`: the blocks of a group stand in increasing adapter order. `gradient_owner_group`: each group owns exactly 4 adapters.
All inputs are finite; a program needn't handle non-finite values.
Results may differ from the reference program's by a relative error of at most 0.0029.
Values may be sent and summed in bfloat16 or wider, within the bound.
No kernel may reach another device: no remote copies, remote signals or barrier semaphores. Data moves between devices by JAX's collectives and lax.ppermute only.
A program may use at most 256 MiB of HBM per device.

```python
import jax
import jax.numpy as jnp
from jax import lax

MODEL_WIDTH = 8192
HIDDEN_UNITS = 16384
ADAPTER_RANK = 16
TENANT_ADAPTERS = 16
BLK = 128
BLOCKS = 8
GROUPS = 4
ROWS = 1024


def layout(key):
    key_one, key_two, key_three, key_four = jax.random.split(key, 4)
    first = jax.random.randint(key_one, (GROUPS, BLOCKS), 0, TENANT_ADAPTERS)
    second = jax.random.randint(key_two, (GROUPS, BLOCKS), 0, TENANT_ADAPTERS)
    relabel = jax.random.permutation(key_three, TENANT_ADAPTERS)
    raw_names = relabel[jnp.minimum(first, second)]
    raw_names = raw_names.at[0].set(TENANT_ADAPTERS - 1)
    names = jnp.sort(raw_names, axis=1)
    per_adapter = jnp.sum((names[:, :, None] == jnp.arange(TENANT_ADAPTERS)[None, None, :]).astype(jnp.int32), axis=1)
    last_fill = jax.random.randint(key_four, (GROUPS, TENANT_ADAPTERS), 1, BLK + 1)
    last_fill = last_fill.at[0, TENANT_ADAPTERS - 1].set(BLK)
    counts = jnp.where(per_adapter > 0, (per_adapter - 1) * BLK + last_fill, 0)
    return (names.astype(jnp.int32), counts.astype(jnp.int32))


def draw_adapter_of_block(key, part):
    return layout(key)[0]


def draw_live_row_counts(key, part):
    return layout(key)[1]


def draw_gradient_owner_group(key, part):
    key = jax.random.fold_in(key, 7)
    shuffled = jax.random.permutation(key, TENANT_ADAPTERS)
    return (shuffled % GROUPS).astype(jnp.int32)


def block_levels(own_key, shape, cuts, smallest, top_value):
    def one(dim, parts):
        heights = jax.random.uniform(jax.random.fold_in(jax.random.fold_in(own_key, 6), dim), (parts,), jnp.float32, smallest / len(cuts), top_value / len(cuts))
        return jnp.repeat(jnp.exp(heights), shape[dim] // parts).reshape((-1,) + (1,) * (len(shape) - dim - 1))

    gain = one(*cuts[0])
    for cut in cuts[1:]:
        gain = gain * one(*cut)
    return gain


def centred(key, dims, spread, reach, cuts=(), kind=jnp.bfloat16):
    entries = jax.random.normal(key, dims, jnp.float32) * spread
    if len(cuts) > 0:
        entries = block_levels(key, dims, cuts, -0.22, 0.18) * entries
    return jnp.clip(entries, min=-reach, max=reach).astype(kind)


def setup_inputs(seed: int = 0, part: int = 0) -> dict:
    streams_of = jax.random.split(jax.random.key(seed), 9)
    part_keys = jax.random.split(jax.random.fold_in(streams_of[8], part), 9)
    return {
        "upstream": centred(part_keys[0], (GROUPS, ROWS, MODEL_WIDTH), 1.0, 6.0, ((0, 4), (1, 4))),
        "hidden": centred(part_keys[1], (GROUPS, ROWS, HIDDEN_UNITS), 1.0, 6.0, ((0, 4), (2, 4))),
        "frozen_weight": centred(streams_of[2], (HIDDEN_UNITS, MODEL_WIDTH), MODEL_WIDTH ** -0.5, 0.0625, ((0, 4),)),
        "adapter_down_factor": centred(part_keys[3], (TENANT_ADAPTERS, ADAPTER_RANK, HIDDEN_UNITS), 0.02, 0.119628906, ((2, 4),)),
        "adapter_up_factor": centred(part_keys[4], (TENANT_ADAPTERS, ADAPTER_RANK, MODEL_WIDTH), 0.02, 0.119628906, ((2, 4),)),
        "live_row_counts": draw_live_row_counts(jax.random.fold_in(jax.random.fold_in(streams_of[8], part), 71), part),
        "adapter_of_block": draw_adapter_of_block(jax.random.fold_in(jax.random.fold_in(streams_of[8], part), 71), part),
        "gradient_owner_group": draw_gradient_owner_group(jax.random.fold_in(jax.random.fold_in(streams_of[8], part), 71), part),
    }


adapter_scale = 2.0


def live_rows(token_blocks, counts):
    count_blocks = token_blocks.shape[0]
    same = token_blocks[:, None] == token_blocks[None, :]
    earlier = jnp.arange(count_blocks, dtype=jnp.int32)[None, :] < jnp.arange(count_blocks, dtype=jnp.int32)[:, None]
    ordinal = jnp.sum((same & earlier).astype(jnp.int32), axis=1)
    hits = token_blocks[:, None] == jnp.arange(counts.shape[0], dtype=jnp.int32)[None, :]
    limit = jnp.sum(jnp.where(hits, counts[None, :], 0), axis=1)
    position = ordinal[:, None] * BLK + jnp.arange(BLK, dtype=jnp.int32)[None, :]
    return position < limit[:, None]


def reference(upstream, hidden, frozen_weight, adapter_down_factor, adapter_up_factor, live_row_counts, adapter_of_block, gradient_owner_group):
    def one_group(items):
        grad_rows, inputs, token_blocks, counts = items
        live = live_rows(token_blocks, counts).reshape(ROWS, 1)
        grad_rows = jnp.where(live, grad_rows, jnp.zeros_like(grad_rows))
        inputs = jnp.where(live, inputs, jnp.zeros_like(inputs))
        base = lax.dot_general(grad_rows, frozen_weight, (((1,), (1,)), ((), ())), preferred_element_type=jnp.float32)
        grad_blk = grad_rows.reshape(BLOCKS, BLK, MODEL_WIDTH).astype(jnp.float32)
        input_blk = inputs.reshape(BLOCKS, BLK, HIDDEN_UNITS).astype(jnp.float32)
        down_factor_block = adapter_down_factor[token_blocks].astype(jnp.float32)
        up_factor_block = adapter_up_factor[token_blocks].astype(jnp.float32)
        lowrank_input = jnp.einsum('bif,brf->bir', input_blk, down_factor_block)
        lowrank_output = jnp.einsum('bik,brk->bir', grad_blk, up_factor_block)
        scaled_input = (adapter_scale * lowrank_input).astype(jnp.bfloat16).astype(jnp.float32)
        scaled_output = (adapter_scale * lowrank_output).astype(jnp.bfloat16).astype(jnp.float32)
        extra = jnp.einsum('bir,brf->bif', scaled_output, down_factor_block).reshape(ROWS, HIDDEN_UNITS)
        result = (base + extra).astype(jnp.bfloat16)
        part_down = jnp.einsum('bir,bif->brf', scaled_output, input_blk)
        part_up = jnp.einsum('bir,bik->brk', scaled_input, grad_blk)
        select = (jnp.arange(TENANT_ADAPTERS, dtype=jnp.int32)[:, None] == token_blocks[None, :]).astype(jnp.float32)
        sum_down = jnp.einsum('ab,brf->arf', select, part_down, precision=lax.Precision.HIGHEST)
        sum_up = jnp.einsum('ab,brk->ark', select, part_up, precision=lax.Precision.HIGHEST)
        return result, sum_down, sum_up

    grad_hidden, parts_down, parts_up = lax.map(one_group, (upstream, hidden, adapter_of_block, live_row_counts))
    total_down = jnp.sum(parts_down, axis=0) * (1.0 / BLK)
    total_up = jnp.sum(parts_up, axis=0) * (1.0 / BLK)
    order = jnp.argsort(gradient_owner_group * TENANT_ADAPTERS + jnp.arange(TENANT_ADAPTERS, dtype=jnp.int32)).astype(jnp.int32)
    return grad_hidden, total_down[order], total_up[order]
```

```python
import functools

import jax
import jax.numpy as jnp
from jax import lax
from jax.experimental import pallas as pl
from jax.experimental.pallas import tpu as pltpu
from jax.sharding import PartitionSpec as P

BLK = 128
SHARD_BLOCKS = 2
SHARES = 4

adapter_scale = 2.0
NT = (((1,), (1,)), ((), ()))
TN = (((0,), (0,)), ((), ()))


def live_counts(token_blocks, counts):
    count_blocks = token_blocks.shape[0]
    same = token_blocks[:, None] == token_blocks[None, :]
    earlier = (
        jnp.arange(count_blocks, dtype=jnp.int32)[None, :]
        < jnp.arange(count_blocks, dtype=jnp.int32)[:, None]
    )
    ordinal = jnp.sum((same & earlier).astype(jnp.int32), axis=1)
    hits = token_blocks[:, None] == jnp.arange(counts.shape[0], dtype=jnp.int32)[None, :]
    limit = jnp.sum(jnp.where(hits, counts[None, :], 0), axis=1)
    return jnp.clip(limit - ordinal * BLK, 0, BLK)


def block_slots(token_blocks, owner):
    adapters = owner.shape[0]
    key = owner * adapters + jnp.arange(adapters, dtype=jnp.int32)
    slot = jnp.sum((key[None, :] < key[:, None]).astype(jnp.int32), axis=1)
    hits = token_blocks[:, None] == jnp.arange(adapters, dtype=jnp.int32)[None, :]
    return jnp.sum(jnp.where(hits, slot[None, :], 0), axis=1)


def product_kernel(npieces, nsrc, has_acc, final, info, *refs):
    sources = refs[: npieces * nsrc]
    rest = list(refs[npieces * nsrc :])
    w_ref = rest.pop(0)
    acc_in = rest.pop(0) if has_acc else None
    if final:
        s_ref, a0_ref, a1_ref, _ = rest[:4]
        rest = rest[4:]
    out_ref, lhs, acc, sems = rest
    f, c = pl.program_id(0), pl.program_id(1)
    last = npieces - 1

    @pl.when((f == 0) & (c == 0))
    def _():
        for i in range(nsrc):

            @pl.when(info[1] == i)
            def _():
                for k in range(npieces):
                    source = sources[i * npieces + k]
                    pltpu.make_async_copy(source, lhs.at[k], sems.at[k]).start()

    for k in range(npieces):

        @pl.when((f == 0) & (c == k))
        def _():
            pltpu.make_async_copy(sources[k], lhs.at[k], sems.at[k]).wait()

    part = lax.dot_general(lhs[c], w_ref[...], NT, preferred_element_type=jnp.float32)

    @pl.when(c == 0)
    def _():
        acc[...] = part + acc_in[...] if has_acc else part

    @pl.when(c > 0)
    def _():
        acc[...] += part

    @pl.when(c == last)
    def _():
        if not final:
            out_ref[...] = acc[...]
        else:
            for b, a_ref in enumerate((a0_ref, a1_ref)):
                rows = slice(b * BLK, (b + 1) * BLK)
                extra = jnp.dot(s_ref[rows, :], a_ref[0], preferred_element_type=jnp.float32)
                base = acc[rows, :]
                live = lax.broadcasted_iota(jnp.int32, base.shape, 0) < info[4 + b]
                out_ref[rows, :] = jnp.where(live, base + extra, 0.0).astype(out_ref.dtype)


def shard_product(info, candidates, weight, first, shares, tile, acc_in=None, final=None):
    nsrc, npieces = len(candidates), len(candidates[0])
    sources = [piece for pieces in candidates for piece in pieces]
    share, width = sources[0].shape
    units = weight.shape[0]

    def weight_map(f, c, info):
        return f, jnp.where(info[1] == 0, first + c, shares - 1 - first - c)

    anyspec = pl.BlockSpec(memory_space=pltpu.HBM)
    args = sources + [weight]
    specs = [anyspec] * len(sources) + [pl.BlockSpec((tile, width), weight_map)]
    if acc_in is not None:
        args.append(acc_in)
        specs.append(pl.BlockSpec((share, tile), lambda f, c, info: (0, f)))
    aliases = {}
    if final is not None:
        scaled, factor, result = final
        rank = scaled.shape[1]
        aliases = {1 + len(args) + 3: 0}
        args += [scaled, factor, factor, result]
        specs += [
            pl.BlockSpec((share, rank), lambda f, c, info: (info[0], 0)),
            pl.BlockSpec((1, rank, tile), lambda f, c, info: (info[2], 0, f)),
            pl.BlockSpec((1, rank, tile), lambda f, c, info: (info[3], 0, f)),
            anyspec,
        ]
        out_shape = jax.ShapeDtypeStruct(result.shape, result.dtype)
        out_spec = pl.BlockSpec((share, tile), lambda f, c, info: (info[0], f))
    else:
        out_shape = jax.ShapeDtypeStruct((share, units), jnp.float32)
        out_spec = pl.BlockSpec((share, tile), lambda f, c, info: (0, f))
    return pl.pallas_call(
        functools.partial(product_kernel, npieces, nsrc, acc_in is not None, final is not None),
        grid_spec=pltpu.PrefetchScalarGridSpec(
            num_scalar_prefetch=1,
            grid=(units // tile, npieces),
            in_specs=specs,
            out_specs=out_spec,
            scratch_shapes=[
                pltpu.VMEM((npieces, share, width), jnp.bfloat16),
                pltpu.VMEM((share, tile), jnp.float32),
                pltpu.SemaphoreType.DMA((npieces,)),
            ],
        ),
        out_shape=out_shape,
        input_output_aliases=aliases,
        compiler_params=pltpu.CompilerParams(
            dimension_semantics=("arbitrary", "arbitrary"), vmem_limit_bytes=40 << 20
        ),
        cost_estimate=pl.CostEstimate(
            flops=2 * share * width * npieces * units,
            bytes_accessed=2 * units * width * npieces,
            transcendentals=0,
        ),
        name="shard_product",
    )(info, *args)


def finish_kernel(info, *refs):
    acc0, acc1, s0, s1, a00, a01, a10, a11, out0_ref = refs
    step = pl.program_id(0)
    for k, (acc, s_ref, factors) in enumerate(((acc0, s0, (a00, a01)), (acc1, s1, (a10, a11)))):

        @pl.when(step == k)
        def _():
            for b, a_ref in enumerate(factors):
                rows = slice(b * BLK, (b + 1) * BLK)
                extra = jnp.dot(s_ref[rows, :], a_ref[0], preferred_element_type=jnp.float32)
                base = acc[rows, :]
                live = lax.broadcasted_iota(jnp.int32, base.shape, 0) < info[k, 4 + b]
                out0_ref[rows, :] = jnp.where(live, base + extra, 0.0).astype(out0_ref.dtype)


def finish_two(info, acc0, acc1, scaled, factor, rows_total, tile):
    share, units = acc0.shape
    rank = scaled.shape[1]
    tiles = units // tile

    def acc_map(k):
        hold = tiles - 1 if k == 0 else 0
        return lambda s, f, info: (0, jnp.where(s == k, f, hold))

    def factor_map(k, b):
        hold = tiles - 1 if k == 0 else 0
        return lambda s, f, info: (info[k, 2 + b], 0, jnp.where(s == k, f, hold))

    return pl.pallas_call(
        finish_kernel,
        grid_spec=pltpu.PrefetchScalarGridSpec(
            num_scalar_prefetch=1,
            grid=(2, tiles),
            in_specs=[
                pl.BlockSpec((share, tile), acc_map(0)),
                pl.BlockSpec((share, tile), acc_map(1)),
                pl.BlockSpec((share, rank), lambda s, f, info: (info[0, 0], 0)),
                pl.BlockSpec((share, rank), lambda s, f, info: (info[1, 0], 0)),
                pl.BlockSpec((1, rank, tile), factor_map(0, 0)),
                pl.BlockSpec((1, rank, tile), factor_map(0, 1)),
                pl.BlockSpec((1, rank, tile), factor_map(1, 0)),
                pl.BlockSpec((1, rank, tile), factor_map(1, 1)),
            ],
            out_specs=pl.BlockSpec((share, tile), lambda s, f, info: (info[s, 0], f)),
        ),
        out_shape=jax.ShapeDtypeStruct((rows_total, units), jnp.bfloat16),
        compiler_params=pltpu.CompilerParams(
            dimension_semantics=("arbitrary", "arbitrary"), vmem_limit_bytes=40 << 20
        ),
        cost_estimate=pl.CostEstimate(
            flops=4 * share * units * rank, bytes_accessed=12 * share * units, transcendentals=0
        ),
        name="finish_two",
    )(info, acc0, acc1, scaled, scaled, factor, factor, factor, factor)


def slice_kernel(n, tri, z_ref, adapters, slots, *refs):
    count = len(tri)
    own = refs[0]
    down = refs[1 : 1 + count]
    up = refs[1 + count : 1 + 2 * count]
    u_ref, s_ref, part_ref, grad_ref, rows_ref, sems = refs[1 + 2 * count :]
    share = rows_ref.shape[0] // n
    width = rows_ref.shape[1]
    z = z_ref[0]

    def each(do):
        for i, (j, c) in enumerate(tri):

            @pl.when(z == c)
            def _():
                do(pltpu.make_async_copy(
                    down[i], rows_ref.at[pl.ds((c + j) * share, share), :], sems.at[j]))

            @pl.when(z == n - 1 - c)
            def _():
                do(pltpu.make_async_copy(
                    up[i], rows_ref.at[pl.ds((n - 1 - c - j) * share, share), :], sems.at[n - 1 + j]))

    def own_copy():
        return pltpu.make_async_copy(
            own.at[:, pl.ds(pl.multiple_of(z * width, width), width)],
            rows_ref.at[pl.ds(pl.multiple_of(z * share, share), share), :],
            sems.at[0],
        )

    own_copy().start()
    each(lambda copy: copy.start())
    own_copy().wait()
    each(lambda copy: copy.wait())
    grad_ref[...] = jnp.zeros_like(grad_ref)
    for b in range(rows_ref.shape[0] // BLK):
        rows = slice(b * BLK, (b + 1) * BLK)
        dy = rows_ref[rows, :]
        part_ref[rows, :] = lax.dot_general(
            dy, u_ref[adapters[b]], NT, preferred_element_type=jnp.float32
        )
        grad_ref[slots[b]] += (1.0 / BLK) * lax.dot_general(
            s_ref[rows, :], dy, TN, preferred_element_type=jnp.float32
        )


def slice_terms(z, adapters, slots, own, down, up, factor, scaled_in, n, tri):
    total = scaled_in.shape[0]
    count_adapters, rank, width = factor.shape
    anyspec = pl.BlockSpec(memory_space=pltpu.HBM)
    vmem = pl.BlockSpec(memory_space=pltpu.VMEM)
    return pl.pallas_call(
        functools.partial(slice_kernel, n, tri),
        grid_spec=pltpu.PrefetchScalarGridSpec(
            num_scalar_prefetch=3,
            grid=(),
            in_specs=[anyspec] * (1 + 2 * len(tri)) + [vmem, vmem],
            out_specs=[vmem, vmem],
            scratch_shapes=[
                pltpu.VMEM((total, width), jnp.bfloat16),
                pltpu.SemaphoreType.DMA((2 * n - 1,)),
            ],
        ),
        out_shape=[
            jax.ShapeDtypeStruct((total, rank), jnp.float32),
            jax.ShapeDtypeStruct((count_adapters, rank, width), jnp.float32),
        ],
        compiler_params=pltpu.CompilerParams(vmem_limit_bytes=40 << 20),
        cost_estimate=pl.CostEstimate(
            flops=4 * total * width * rank,
            bytes_accessed=2 * total * width + 6 * count_adapters * rank * width,
            transcendentals=0,
        ),
        name="slice_terms",
    )(z, adapters, slots, own, *down, *up, factor, scaled_in)


def down_kernel(slots, s_ref, x_ref, grad_ref):
    grad_ref[...] = jnp.zeros_like(grad_ref)
    for b in range(x_ref.shape[0] // BLK):
        rows = slice(b * BLK, (b + 1) * BLK)
        grad_ref[slots[b]] += (1.0 / BLK) * lax.dot_general(
            s_ref[rows, :], x_ref[rows, :], TN, preferred_element_type=jnp.float32
        )


def down_terms(slots, scaled_out, inputs, count_adapters, tile):
    total, units = inputs.shape
    rank = scaled_out.shape[1]
    return pl.pallas_call(
        down_kernel,
        grid_spec=pltpu.PrefetchScalarGridSpec(
            num_scalar_prefetch=1,
            grid=(units // tile,),
            in_specs=[
                pl.BlockSpec((total, rank), lambda f, slots: (0, 0)),
                pl.BlockSpec((total, tile), lambda f, slots: (0, f)),
            ],
            out_specs=pl.BlockSpec((count_adapters, rank, tile), lambda f, slots: (0, 0, f)),
        ),
        out_shape=jax.ShapeDtypeStruct((count_adapters, rank, units), jnp.float32),
        compiler_params=pltpu.CompilerParams(
            dimension_semantics=("arbitrary",), vmem_limit_bytes=40 << 20
        ),
        cost_estimate=pl.CostEstimate(
            flops=2 * total * units * rank,
            bytes_accessed=2 * total * units + 4 * count_adapters * rank * units,
            transcendentals=0,
        ),
        name="down_terms",
    )(slots, scaled_out, inputs)


def on_line(
    upstream,
    hidden,
    frozen_weight,
    adapter_down_factor,
    adapter_up_factor,
    live_row_counts,
    adapter_of_block,
    gradient_owner_group,
):
    n = SHARES
    z = lax.axis_index("tp")
    own = upstream[0]
    share, features = own.shape
    width = features // n
    total = share * n
    units = hidden.shape[2]
    adapters = gradient_owner_group.shape[0]

    down = [[own[:, c * width : (c + 1) * width] for c in range(n)]]
    up = [[down[0][n - 1 - c] for c in range(n)]]
    for j in range(1, n):
        to_lower = [(s, s - 1) for s in range(1, n) if s + j - 1 < n]
        to_upper = [(s, s + 1) for s in range(n - 1) if s - j + 1 >= 0]
        down.append([lax.ppermute(down[j - 1][c], "tp", to_lower) for c in range(n)])
        up.append([lax.ppermute(up[j - 1][c], "tp", to_upper) for c in range(n)])

    token_blocks = adapter_of_block[0]
    counts = live_counts(token_blocks, live_row_counts[0])
    slots = block_slots(token_blocks, gradient_owner_group)
    live = (
        jnp.arange(BLK, dtype=jnp.int32)[None, :] < counts[:, None]
    ).reshape(total)[:, None]

    inputs = hidden[0]
    part_in = jnp.einsum(
        "bif,brf->bir",
        inputs.reshape(-1, BLK, units),
        adapter_down_factor[token_blocks],
        preferred_element_type=jnp.float32,
    ).reshape(total, -1)
    low_in = lax.psum(part_in, "tp")
    scaled_in = jnp.where(live, adapter_scale * low_in, 0.0).astype(jnp.bfloat16)

    tri = [(j, c) for j in range(1, n) for c in range(n - j)]
    part_out, slot_up = slice_terms(
        z.reshape(1).astype(jnp.int32), token_blocks, slots, own,
        [down[j][c] for j, c in tri], [up[j][c] for j, c in tri],
        adapter_up_factor, scaled_in, n, tri,
    )
    low_out = lax.psum(part_out, "tp")
    scaled_out = jnp.where(live, adapter_scale * low_out, 0.0).astype(jnp.bfloat16)
    slot_down = down_terms(slots, scaled_out, inputs, adapters, 1024)
    grad_up = lax.psum_scatter(slot_up, "dp", scatter_dimension=0, tiled=True)
    grad_down = lax.psum_scatter(slot_down, "dp", scatter_dimension=0, tiled=True)

    def info_of(shard, candidate):
        pair = shard * SHARD_BLOCKS + jnp.arange(SHARD_BLOCKS, dtype=jnp.int32)
        hits = pair[:, None] == jnp.arange(token_blocks.shape[0], dtype=jnp.int32)[None, :]
        names = jnp.sum(jnp.where(hits, token_blocks[None, :], 0), axis=1)
        lives = jnp.sum(jnp.where(hits, counts[None, :], 0), axis=1)
        head = jnp.stack([shard, candidate]).astype(jnp.int32)
        return jnp.concatenate([head, names, lives])

    infos = [info_of(z, jnp.zeros((), jnp.int32))]
    for k in range(1, n):
        step_up = jnp.maximum(k - (n - 1 - z), 0)
        infos.append(info_of(jnp.where(step_up == 0, z + k, z - step_up), step_up))

    def candidates(k, lo, hi):
        return [down[k][lo:hi]] + [up[j][lo:hi] for j in range(1, k + 1)]

    tile = 1024
    acc_own = shard_product(infos[0], [down[0]], frozen_weight, 0, n, tile)
    acc_one = shard_product(infos[1], candidates(1, 0, n), frozen_weight, 0, n, tile)
    result = finish_two(
        jnp.stack(infos[:2]), acc_own, acc_one, scaled_out, adapter_down_factor, total, tile
    )
    result = shard_product(
        infos[2], candidates(2, 0, n), frozen_weight, 0, n, tile,
        final=(scaled_out, adapter_down_factor, result),
    )
    acc_last = shard_product(infos[3], candidates(3, 0, n - 1), frozen_weight, 0, n, tile)
    result = shard_product(
        infos[3], candidates(3, n - 1, n), frozen_weight, n - 1, n, tile, acc_in=acc_last,
        final=(scaled_out, adapter_down_factor, result),
    )
    return (result[None], grad_down, grad_up)


def gathered(
    upstream,
    hidden,
    frozen_weight,
    adapter_down_factor,
    adapter_up_factor,
    live_row_counts,
    adapter_of_block,
    gradient_owner_group,
):
    token_blocks = adapter_of_block[0]
    counts = live_counts(token_blocks, live_row_counts[0])
    slots = block_slots(token_blocks, gradient_owner_group)
    live = jnp.arange(BLK, dtype=jnp.int32)[None, :, None] < counts[:, None, None]
    inputs = hidden[0].reshape(-1, BLK, hidden.shape[2])
    down_factor = adapter_down_factor[token_blocks]
    local = adapter_up_factor.shape[2]
    grad_rows = lax.all_gather(upstream[0], "tp", axis=0, tiled=True)
    grad_slice = lax.dynamic_slice_in_dim(grad_rows, lax.axis_index("tp") * local, local, 1)
    grad_blk = grad_slice.reshape(-1, BLK, local)
    dot = functools.partial(jnp.einsum, preferred_element_type=jnp.float32)
    low_in, low_out = lax.psum(
        (
            dot("bif,brf->bir", inputs, down_factor),
            dot("bik,brk->bir", grad_blk, adapter_up_factor[token_blocks]),
        ),
        "tp",
    )
    scaled_in = jnp.where(live, adapter_scale * low_in, 0.0).astype(jnp.bfloat16)
    scaled_out = jnp.where(live, adapter_scale * low_out, 0.0).astype(jnp.bfloat16)
    base = lax.dot_general(grad_rows, frozen_weight, NT, preferred_element_type=jnp.float32)
    extra = dot("bir,brf->bif", scaled_out, down_factor)
    result = jnp.where(live, base.reshape(extra.shape) + extra, 0.0).astype(jnp.bfloat16)
    names = jnp.arange(gradient_owner_group.shape[0], dtype=jnp.int32)
    select = (names[:, None] == slots[None, :]).astype(jnp.float32)
    exact = functools.partial(jnp.einsum, precision=lax.Precision.HIGHEST)
    slot_down = exact("sb,brf->srf", select, dot("bir,bif->brf", scaled_out, inputs))
    slot_up = exact("sb,brk->srk", select, dot("bir,bik->brk", scaled_in, grad_blk))
    owned_down = lax.psum_scatter(slot_down, "dp", scatter_dimension=0, tiled=True)
    owned_up = lax.psum_scatter(slot_up, "dp", scatter_dimension=0, tiled=True)
    result = result.reshape(1, grad_rows.shape[0], -1)
    return (result, owned_down * (1.0 / BLK), owned_up * (1.0 / BLK))


def solution(mesh):
    return jax.shard_map(
        on_line if mesh.shape["tp"] == SHARES else gathered,
        mesh=mesh,
        in_specs=(
            P(("rep", "dp"), "tp", None),
            P(("rep", "dp"), None, "tp"),
            P("tp", None),
            P("rep", None, "tp"),
            P("rep", None, "tp"),
            P(("rep", "dp"), None),
            P(("rep", "dp"), None),
            P("rep"),
        ),
        out_specs=(
            P(("rep", "dp"), None, "tp"),
            P(("rep", "dp"), None, "tp"),
            P(("rep", "dp"), None, "tp"),
        ),
        check_vma=False,
    )
```

```python
import functools

import jax
import jax.numpy as jnp
from jax import lax
from jax.experimental import pallas as pl
from jax.experimental.pallas import tpu as pltpu
from jax.sharding import PartitionSpec as P

BLK = 128
SHARD_BLOCKS = 2
SHARES = 4

adapter_scale = 2.0
NT = (((1,), (1,)), ((), ()))
TN = (((0,), (0,)), ((), ()))


def live_counts(token_blocks, counts):
    count_blocks = token_blocks.shape[0]
    same = token_blocks[:, None] == token_blocks[None, :]
    earlier = (
        jnp.arange(count_blocks, dtype=jnp.int32)[None, :]
        < jnp.arange(count_blocks, dtype=jnp.int32)[:, None]
    )
    ordinal = jnp.sum((same & earlier).astype(jnp.int32), axis=1)
    hits = token_blocks[:, None] == jnp.arange(counts.shape[0], dtype=jnp.int32)[None, :]
    limit = jnp.sum(jnp.where(hits, counts[None, :], 0), axis=1)
    return jnp.clip(limit - ordinal * BLK, 0, BLK)


def block_slots(token_blocks, owner):
    adapters = owner.shape[0]
    key = owner * adapters + jnp.arange(adapters, dtype=jnp.int32)
    slot = jnp.sum((key[None, :] < key[:, None]).astype(jnp.int32), axis=1)
    hits = token_blocks[:, None] == jnp.arange(adapters, dtype=jnp.int32)[None, :]
    return jnp.sum(jnp.where(hits, slot[None, :], 0), axis=1)


def product_kernel(npieces, nsrc, has_acc, final, info, *refs):
    sources = refs[: npieces * nsrc]
    rest = list(refs[npieces * nsrc :])
    w_ref = rest.pop(0)
    acc_in = rest.pop(0) if has_acc else None
    if final:
        s_ref, a0_ref, a1_ref, _ = rest[:4]
        rest = rest[4:]
    out_ref, lhs, turned, acc, sems = rest
    f, c = pl.program_id(0), pl.program_id(1)
    last = npieces - 1

    @pl.when((f == 0) & (c == 0))
    def _():
        for i in range(nsrc):

            @pl.when(info[1] == i)
            def _():
                for k in range(npieces):
                    source = sources[i * npieces + k]
                    pltpu.make_async_copy(source, lhs.at[k], sems.at[k]).start()

    for k in range(npieces):

        @pl.when((f == 0) & (c == k))
        def _():
            pltpu.make_async_copy(sources[k], lhs.at[k], sems.at[k]).wait()
            turned[k] = lhs[k].T

    part = jnp.dot(w_ref[...], turned[c], preferred_element_type=jnp.float32)

    @pl.when(c == 0)
    def _():
        acc[...] = part + acc_in[...] if has_acc else part

    @pl.when(c > 0)
    def _():
        acc[...] += part

    @pl.when(c == last)
    def _():
        if final:
            finish_rows(acc, s_ref, (a0_ref, a1_ref), (info[4], info[5]), out_ref)
        else:
            out_ref[...] = acc[...]


def finish_rows(acc, s_ref, factors, lives, out_ref):
    for b, a_ref in enumerate(factors):
        rows = slice(b * BLK, (b + 1) * BLK)
        extra = jnp.dot(s_ref[rows, :], a_ref[0], preferred_element_type=jnp.float32)
        base = acc[:, rows].T
        live = lax.broadcasted_iota(jnp.int32, base.shape, 0) < lives[b]
        out_ref[rows, :] = jnp.where(live, base + extra, 0.0).astype(out_ref.dtype)


def shard_product(info, candidates, weight, first, shares, tile, acc_in=None, final=None):
    nsrc, npieces = len(candidates), len(candidates[0])
    sources = [piece for pieces in candidates for piece in pieces]
    share, width = sources[0].shape
    units = weight.shape[0]

    def weight_map(f, c, info):
        return f, jnp.where(info[1] == 0, first + c, shares - 1 - first - c)

    anyspec = pl.BlockSpec(memory_space=pltpu.HBM)
    args = sources + [weight]
    specs = [anyspec] * len(sources) + [pl.BlockSpec((tile, width), weight_map)]
    if acc_in is not None:
        args.append(acc_in)
        specs.append(pl.BlockSpec((tile, share), lambda f, c, info: (f, 0)))
    aliases = {}
    if final is not None:
        scaled, factor, result = final
        rank = scaled.shape[1]
        aliases = {1 + len(args) + 3: 0}
        args += [scaled, factor, factor, result]
        specs += [
            pl.BlockSpec((share, rank), lambda f, c, info: (info[0], 0)),
            pl.BlockSpec((1, rank, tile), lambda f, c, info: (info[2], 0, f)),
            pl.BlockSpec((1, rank, tile), lambda f, c, info: (info[3], 0, f)),
            anyspec,
        ]
        out_shape = jax.ShapeDtypeStruct(result.shape, result.dtype)
        out_spec = pl.BlockSpec((share, tile), lambda f, c, info: (info[0], f))
    else:
        out_shape = jax.ShapeDtypeStruct((units, share), jnp.float32)
        out_spec = pl.BlockSpec((tile, share), lambda f, c, info: (f, 0))
    return pl.pallas_call(
        functools.partial(product_kernel, npieces, nsrc, acc_in is not None, final is not None),
        grid_spec=pltpu.PrefetchScalarGridSpec(
            num_scalar_prefetch=1,
            grid=(units // tile, npieces),
            in_specs=specs,
            out_specs=out_spec,
            scratch_shapes=[
                pltpu.VMEM((npieces, share, width), jnp.bfloat16),
                pltpu.VMEM((npieces, width, share), jnp.bfloat16),
                pltpu.VMEM((tile, share), jnp.float32),
                pltpu.SemaphoreType.DMA((npieces,)),
            ],
        ),
        out_shape=out_shape,
        input_output_aliases=aliases,
        compiler_params=pltpu.CompilerParams(
            dimension_semantics=("arbitrary", "arbitrary"), vmem_limit_bytes=40 << 20
        ),
        cost_estimate=pl.CostEstimate(
            flops=2 * share * width * npieces * units,
            bytes_accessed=2 * units * width * npieces,
            transcendentals=0,
        ),
        name="shard_product",
    )(info, *args)


def finish_kernel(info, *refs):
    acc0, acc1, s0, s1, a00, a01, a10, a11, out_ref = refs
    step = pl.program_id(0)
    for k, (acc, s_ref, factors) in enumerate(((acc0, s0, (a00, a01)), (acc1, s1, (a10, a11)))):

        @pl.when(step == k)
        def _():
            finish_rows(acc, s_ref, factors, (info[k, 4], info[k, 5]), out_ref)


def finish_two(info, acc0, acc1, scaled, factor, rows_total, tile):
    units, share = acc0.shape
    rank = scaled.shape[1]
    tiles = units // tile

    def acc_map(k):
        hold = tiles - 1 if k == 0 else 0
        return lambda s, f, info: (jnp.where(s == k, f, hold), 0)

    def factor_map(k, b):
        hold = tiles - 1 if k == 0 else 0
        return lambda s, f, info: (info[k, 2 + b], 0, jnp.where(s == k, f, hold))

    return pl.pallas_call(
        finish_kernel,
        grid_spec=pltpu.PrefetchScalarGridSpec(
            num_scalar_prefetch=1,
            grid=(2, tiles),
            in_specs=[
                pl.BlockSpec((tile, share), acc_map(0)),
                pl.BlockSpec((tile, share), acc_map(1)),
                pl.BlockSpec((share, rank), lambda s, f, info: (info[0, 0], 0)),
                pl.BlockSpec((share, rank), lambda s, f, info: (info[1, 0], 0)),
                pl.BlockSpec((1, rank, tile), factor_map(0, 0)),
                pl.BlockSpec((1, rank, tile), factor_map(0, 1)),
                pl.BlockSpec((1, rank, tile), factor_map(1, 0)),
                pl.BlockSpec((1, rank, tile), factor_map(1, 1)),
            ],
            out_specs=pl.BlockSpec((share, tile), lambda s, f, info: (info[s, 0], f)),
        ),
        out_shape=jax.ShapeDtypeStruct((rows_total, units), jnp.bfloat16),
        compiler_params=pltpu.CompilerParams(
            dimension_semantics=("arbitrary", "arbitrary"), vmem_limit_bytes=40 << 20
        ),
        cost_estimate=pl.CostEstimate(
            flops=4 * share * units * rank, bytes_accessed=12 * share * units, transcendentals=0
        ),
        name="finish_two",
    )(info, acc0, acc1, scaled, scaled, factor, factor, factor, factor)


def slice_kernel(n, tri, z_ref, adapters, slots, *refs):
    count = len(tri)
    own = refs[0]
    down = refs[1 : 1 + count]
    up = refs[1 + count : 1 + 2 * count]
    u_ref, s_ref, part_ref, grad_ref, rows_ref, sems = refs[1 + 2 * count :]
    share = rows_ref.shape[0] // n
    width = rows_ref.shape[1]
    z = z_ref[0]

    def each(do):
        for i, (j, c) in enumerate(tri):

            @pl.when(z == c)
            def _():
                do(pltpu.make_async_copy(
                    down[i], rows_ref.at[pl.ds((c + j) * share, share), :], sems.at[j]))

            @pl.when(z == n - 1 - c)
            def _():
                do(pltpu.make_async_copy(
                    up[i], rows_ref.at[pl.ds((n - 1 - c - j) * share, share), :], sems.at[n - 1 + j]))

    def own_copy():
        return pltpu.make_async_copy(
            own.at[:, pl.ds(pl.multiple_of(z * width, width), width)],
            rows_ref.at[pl.ds(pl.multiple_of(z * share, share), share), :],
            sems.at[0],
        )

    own_copy().start()
    each(lambda copy: copy.start())
    own_copy().wait()
    each(lambda copy: copy.wait())
    grad_ref[...] = jnp.zeros_like(grad_ref)
    for b in range(rows_ref.shape[0] // BLK):
        rows = slice(b * BLK, (b + 1) * BLK)
        dy = rows_ref[rows, :]
        part_ref[rows, :] = lax.dot_general(
            dy, u_ref[adapters[b]], NT, preferred_element_type=jnp.float32
        )
        grad_ref[slots[b]] += (1.0 / BLK) * lax.dot_general(
            s_ref[rows, :], dy, TN, preferred_element_type=jnp.float32
        )


def slice_terms(z, adapters, slots, own, down, up, factor, scaled_in, n, tri):
    total = scaled_in.shape[0]
    count_adapters, rank, width = factor.shape
    anyspec = pl.BlockSpec(memory_space=pltpu.HBM)
    vmem = pl.BlockSpec(memory_space=pltpu.VMEM)
    return pl.pallas_call(
        functools.partial(slice_kernel, n, tri),
        grid_spec=pltpu.PrefetchScalarGridSpec(
            num_scalar_prefetch=3,
            grid=(),
            in_specs=[anyspec] * (1 + 2 * len(tri)) + [vmem, vmem],
            out_specs=[vmem, vmem],
            scratch_shapes=[
                pltpu.VMEM((total, width), jnp.bfloat16),
                pltpu.SemaphoreType.DMA((2 * n - 1,)),
            ],
        ),
        out_shape=[
            jax.ShapeDtypeStruct((total, rank), jnp.float32),
            jax.ShapeDtypeStruct((count_adapters, rank, width), jnp.float32),
        ],
        compiler_params=pltpu.CompilerParams(vmem_limit_bytes=40 << 20),
        cost_estimate=pl.CostEstimate(
            flops=4 * total * width * rank,
            bytes_accessed=2 * total * width + 6 * count_adapters * rank * width,
            transcendentals=0,
        ),
        name="slice_terms",
    )(z, adapters, slots, own, *down, *up, factor, scaled_in)


def down_kernel(slots, s_ref, x_ref, grad_ref):
    grad_ref[...] = jnp.zeros_like(grad_ref)
    for b in range(x_ref.shape[0] // BLK):
        rows = slice(b * BLK, (b + 1) * BLK)
        grad_ref[slots[b]] += (1.0 / BLK) * lax.dot_general(
            s_ref[rows, :], x_ref[rows, :], TN, preferred_element_type=jnp.float32
        )


def down_terms(slots, scaled_out, inputs, count_adapters, tile):
    total, units = inputs.shape
    rank = scaled_out.shape[1]
    return pl.pallas_call(
        down_kernel,
        grid_spec=pltpu.PrefetchScalarGridSpec(
            num_scalar_prefetch=1,
            grid=(units // tile,),
            in_specs=[
                pl.BlockSpec((total, rank), lambda f, slots: (0, 0)),
                pl.BlockSpec((total, tile), lambda f, slots: (0, f)),
            ],
            out_specs=pl.BlockSpec((count_adapters, rank, tile), lambda f, slots: (0, 0, f)),
        ),
        out_shape=jax.ShapeDtypeStruct((count_adapters, rank, units), jnp.float32),
        compiler_params=pltpu.CompilerParams(
            dimension_semantics=("arbitrary",), vmem_limit_bytes=40 << 20
        ),
        cost_estimate=pl.CostEstimate(
            flops=2 * total * units * rank,
            bytes_accessed=2 * total * units + 4 * count_adapters * rank * units,
            transcendentals=0,
        ),
        name="down_terms",
    )(slots, scaled_out, inputs)


def on_line(
    upstream,
    hidden,
    frozen_weight,
    adapter_down_factor,
    adapter_up_factor,
    live_row_counts,
    adapter_of_block,
    gradient_owner_group,
):
    n = SHARES
    z = lax.axis_index("tp")
    own = upstream[0]
    share, features = own.shape
    width = features // n
    total = share * n
    units = hidden.shape[2]
    adapters = gradient_owner_group.shape[0]

    token_blocks = adapter_of_block[0]
    counts = live_counts(token_blocks, live_row_counts[0])
    slots = block_slots(token_blocks, gradient_owner_group)
    live = (
        jnp.arange(BLK, dtype=jnp.int32)[None, :] < counts[:, None]
    ).reshape(total)[:, None]
    inputs = hidden[0]

    def info_of(shard, candidate):
        pair = shard * SHARD_BLOCKS + jnp.arange(SHARD_BLOCKS, dtype=jnp.int32)
        hits = pair[:, None] == jnp.arange(token_blocks.shape[0], dtype=jnp.int32)[None, :]
        names = jnp.sum(jnp.where(hits, token_blocks[None, :], 0), axis=1)
        lives = jnp.sum(jnp.where(hits, counts[None, :], 0), axis=1)
        head = jnp.stack([shard, candidate]).astype(jnp.int32)
        return jnp.concatenate([head, names, lives])

    infos = [info_of(z, jnp.zeros((), jnp.int32))]
    for k in range(1, n):
        step_up = jnp.maximum(k - (n - 1 - z), 0)
        infos.append(info_of(jnp.where(step_up == 0, z + k, z - step_up), step_up))

    down = [[own[:, c * width : (c + 1) * width] for c in range(n)]]
    up = [[down[0][n - 1 - c] for c in range(n)]]
    down += [[None] * n for _ in range(1, n)]
    up += [[None] * n for _ in range(1, n)]

    def send(place, *after):
        j, c = place
        to_lower = [(s, s - 1) for s in range(1, n) if s + j - 1 < n]
        to_upper = [(s, s + 1) for s in range(n - 1) if s - j + 1 >= 0]
        low, high = held((down[j - 1][c], up[j - 1][c]), *after)
        down[j][c] = lax.ppermute(low, "tp", to_lower)
        up[j][c] = lax.ppermute(high, "tp", to_upper)

    def held(value, *after):
        return lax.optimization_barrier((value, after))[0] if after else value

    def came(place):
        j, c = place
        return (down[j][c], up[j][c])

    def candidates(k, lo, hi):
        return [down[k][lo:hi]] + [up[j][lo:hi] for j in range(1, k + 1)]

    order = [
        (1, 0), (1, 1), (1, 2), (2, 0), (2, 1), (1, 3),
        (3, 0), (2, 2), (3, 1), (2, 3), (3, 2), (3, 3),
    ]
    tri = [(j, c) for j in range(1, n) for c in range(n - j)]
    tile = 1024

    for place in order[:3]:
        send(place)
    part_in = jnp.einsum(
        "bif,brf->bir",
        inputs.reshape(-1, BLK, units),
        adapter_down_factor[token_blocks],
        preferred_element_type=jnp.float32,
    ).reshape(total, -1)
    low_in = lax.psum(part_in, "tp")
    send(order[3], came(order[0]), part_in)
    acc_own = shard_product(
        held(infos[0], came(order[0])), [down[0]], frozen_weight, 0, n, tile
    )
    send(order[4], came(order[1]), acc_own)
    scaled_in = jnp.where(live, adapter_scale * low_in, 0.0).astype(jnp.bfloat16)
    send(order[5], came(order[2]), scaled_in)
    send(order[6], came(order[3]))
    send(order[7], came(order[4]))
    acc_one = shard_product(
        held(infos[1], came(order[5])), candidates(1, 0, n), frozen_weight, 0, n, tile
    )
    send(order[8], came(order[5]), acc_one)
    part_out, slot_up = slice_terms(
        z.reshape(1).astype(jnp.int32), token_blocks, slots, own,
        [down[j][c] for j, c in tri], [up[j][c] for j, c in tri],
        adapter_up_factor, scaled_in, n, tri,
    )
    send(order[9], came(order[6]), part_out)
    low_out = lax.psum(part_out, "tp")
    grad_up = lax.psum_scatter(slot_up, "dp", scatter_dimension=0, tiled=True)
    send(order[10], came(order[7]))
    low_out = held(low_out, came(order[8]))
    scaled_out = jnp.where(live, adapter_scale * low_out, 0.0).astype(jnp.bfloat16)
    slot_down = down_terms(slots, scaled_out, inputs, adapters, 1024)
    send(order[11], came(order[8]), slot_down)
    grad_down = lax.psum_scatter(slot_down, "dp", scatter_dimension=0, tiled=True)
    result = finish_two(
        jnp.stack(infos[:2]), acc_own, acc_one, scaled_out, adapter_down_factor, total, tile
    )
    result = shard_product(
        infos[2], candidates(2, 0, n), frozen_weight, 0, n, tile,
        final=(scaled_out, adapter_down_factor, result),
    )
    acc_last = shard_product(infos[3], candidates(3, 0, n - 1), frozen_weight, 0, n, tile)
    result = shard_product(
        infos[3], candidates(3, n - 1, n), frozen_weight, n - 1, n, tile, acc_in=acc_last,
        final=(scaled_out, adapter_down_factor, result),
    )
    return (result[None], grad_down, grad_up)


def gathered(
    upstream,
    hidden,
    frozen_weight,
    adapter_down_factor,
    adapter_up_factor,
    live_row_counts,
    adapter_of_block,
    gradient_owner_group,
):
    token_blocks = adapter_of_block[0]
    counts = live_counts(token_blocks, live_row_counts[0])
    slots = block_slots(token_blocks, gradient_owner_group)
    live = jnp.arange(BLK, dtype=jnp.int32)[None, :, None] < counts[:, None, None]
    inputs = hidden[0].reshape(-1, BLK, hidden.shape[2])
    down_factor = adapter_down_factor[token_blocks]
    local = adapter_up_factor.shape[2]
    grad_rows = lax.all_gather(upstream[0], "tp", axis=0, tiled=True)
    grad_slice = lax.dynamic_slice_in_dim(grad_rows, lax.axis_index("tp") * local, local, 1)
    grad_blk = grad_slice.reshape(-1, BLK, local)
    dot = functools.partial(jnp.einsum, preferred_element_type=jnp.float32)
    low_in, low_out = lax.psum(
        (
            dot("bif,brf->bir", inputs, down_factor),
            dot("bik,brk->bir", grad_blk, adapter_up_factor[token_blocks]),
        ),
        "tp",
    )
    scaled_in = jnp.where(live, adapter_scale * low_in, 0.0).astype(jnp.bfloat16)
    scaled_out = jnp.where(live, adapter_scale * low_out, 0.0).astype(jnp.bfloat16)
    base = lax.dot_general(grad_rows, frozen_weight, NT, preferred_element_type=jnp.float32)
    extra = dot("bir,brf->bif", scaled_out, down_factor)
    result = jnp.where(live, base.reshape(extra.shape) + extra, 0.0).astype(jnp.bfloat16)
    names = jnp.arange(gradient_owner_group.shape[0], dtype=jnp.int32)
    select = (names[:, None] == slots[None, :]).astype(jnp.float32)
    exact = functools.partial(jnp.einsum, precision=lax.Precision.HIGHEST)
    slot_down = exact("sb,brf->srf", select, dot("bir,bif->brf", scaled_out, inputs))
    slot_up = exact("sb,brk->srk", select, dot("bir,bik->brk", scaled_in, grad_blk))
    owned_down = lax.psum_scatter(slot_down, "dp", scatter_dimension=0, tiled=True)
    owned_up = lax.psum_scatter(slot_up, "dp", scatter_dimension=0, tiled=True)
    result = result.reshape(1, grad_rows.shape[0], -1)
    return (result, owned_down * (1.0 / BLK), owned_up * (1.0 / BLK))


def solution(mesh):
    return jax.shard_map(
        on_line if mesh.shape["tp"] == SHARES else gathered,
        mesh=mesh,
        in_specs=(
            P(("rep", "dp"), "tp", None),
            P(("rep", "dp"), None, "tp"),
            P("tp", None),
            P("rep", None, "tp"),
            P("rep", None, "tp"),
            P(("rep", "dp"), None),
            P(("rep", "dp"), None),
            P("rep"),
        ),
        out_specs=(
            P(("rep", "dp"), None, "tp"),
            P(("rep", "dp"), None, "tp"),
            P(("rep", "dp"), None, "tp"),
        ),
        check_vma=False,
    )
```

```python
import functools

import jax
import jax.numpy as jnp
from jax import lax
from jax.experimental import pallas as pl
from jax.experimental.pallas import tpu as pltpu
from jax.sharding import PartitionSpec as P

BLK = 128
SHARD_BLOCKS = 2
SHARES = 4
VMEM_BYTES = 60 << 20
RING = 4

adapter_scale = 2.0
NT = (((1,), (1,)), ((), ()))
TN = (((0,), (0,)), ((), ()))


def live_counts(token_blocks, counts):
    count_blocks = token_blocks.shape[0]
    same = token_blocks[:, None] == token_blocks[None, :]
    earlier = (
        jnp.arange(count_blocks, dtype=jnp.int32)[None, :]
        < jnp.arange(count_blocks, dtype=jnp.int32)[:, None]
    )
    ordinal = jnp.sum((same & earlier).astype(jnp.int32), axis=1)
    hits = token_blocks[:, None] == jnp.arange(counts.shape[0], dtype=jnp.int32)[None, :]
    limit = jnp.sum(jnp.where(hits, counts[None, :], 0), axis=1)
    return jnp.clip(limit - ordinal * BLK, 0, BLK)


def block_slots(token_blocks, owner):
    adapters = owner.shape[0]
    key = owner * adapters + jnp.arange(adapters, dtype=jnp.int32)
    slot = jnp.sum((key[None, :] < key[:, None]).astype(jnp.int32), axis=1)
    hits = token_blocks[:, None] == jnp.arange(adapters, dtype=jnp.int32)[None, :]
    return jnp.sum(jnp.where(hits, slot[None, :], 0), axis=1)


def product_kernel(npieces, nsrc, has_acc, final, first, shares, info, *refs):
    sources = refs[: npieces * nsrc]
    rest = list(refs[npieces * nsrc :])
    w_ref = rest.pop(0)
    acc_in = rest.pop(0) if has_acc else None
    if final:
        s_ref, a0_ref, a1_ref, _ = rest[:4]
        rest = rest[4:]
    out_ref, weights, lhs, turned, acc, sems, weight_sems = rest
    f, c = pl.program_id(0), pl.program_id(1)
    last = npieces - 1
    ring, tile, width = weights.shape
    step = f * npieces + c
    steps = pl.num_programs(0) * npieces

    def weight_copy(t):
        k = first + lax.rem(t, npieces)
        column = jnp.where(info[1] == 0, k, shares - 1 - k) * width
        block = w_ref.at[
            pl.ds(pl.multiple_of(lax.div(t, npieces) * tile, tile), tile),
            pl.ds(pl.multiple_of(column, width), width),
        ]
        slot = lax.rem(t, ring)
        return pltpu.make_async_copy(block, weights.at[slot], weight_sems.at[slot])

    @pl.when(step == 0)
    def _():
        for i in range(nsrc):

            @pl.when(info[1] == i)
            def _():
                for k in range(npieces):
                    source = sources[i * npieces + k]
                    pltpu.make_async_copy(source, lhs.at[k], sems.at[k]).start()

        for t in range(ring):
            weight_copy(t).start()

    @pl.when((step > 0) & (step + ring - 1 < steps))
    def _():
        weight_copy(step + ring - 1).start()

    for k in range(npieces):

        @pl.when((f == 0) & (c == k))
        def _():
            pltpu.make_async_copy(sources[k], lhs.at[k], sems.at[k]).wait()
            turned[k] = lhs[k].T

    weight_copy(step).wait()
    part = jnp.dot(
        weights[lax.rem(step, ring)], turned[c], preferred_element_type=jnp.float32
    )

    @pl.when(c == 0)
    def _():
        acc[...] = part + acc_in[...] if has_acc else part

    @pl.when(c > 0)
    def _():
        acc[...] += part

    @pl.when(c == last)
    def _():
        if final:
            finish_rows(acc, s_ref, (a0_ref, a1_ref), (info[4], info[5]), out_ref)
        else:
            out_ref[...] = acc[...]


def finish_rows(acc, s_ref, factors, lives, out_ref):
    for b, a_ref in enumerate(factors):
        rows = slice(b * BLK, (b + 1) * BLK)
        extra = lax.dot_general(s_ref[b], a_ref[0], TN, preferred_element_type=jnp.float32)
        base = acc[:, rows].T
        live = lax.broadcasted_iota(jnp.int32, base.shape, 0) < lives[b]
        out_ref[rows, :] = jnp.where(live, base + extra, 0.0).astype(out_ref.dtype)


def shard_product(info, candidates, weight, first, shares, tile, acc_in=None, final=None):
    nsrc, npieces = len(candidates), len(candidates[0])
    sources = [piece for pieces in candidates for piece in pieces]
    share, width = sources[0].shape
    units = weight.shape[0]

    anyspec = pl.BlockSpec(memory_space=pltpu.HBM)
    args = sources + [weight]
    specs = [anyspec] * (len(sources) + 1)
    if acc_in is not None:
        args.append(acc_in)
        specs.append(pl.BlockSpec((tile, share), lambda f, c, info: (f, 0)))
    aliases = {}
    if final is not None:
        scaled, factor, result = final
        rank = scaled.shape[1]
        aliases = {1 + len(args) + 3: 0}
        args += [scaled, factor, factor, result]
        specs += [
            pl.BlockSpec((SHARD_BLOCKS, rank, BLK), lambda f, c, info: (info[0], 0, 0)),
            pl.BlockSpec((1, rank, tile), lambda f, c, info: (info[2], 0, f)),
            pl.BlockSpec((1, rank, tile), lambda f, c, info: (info[3], 0, f)),
            anyspec,
        ]
        out_shape = jax.ShapeDtypeStruct(result.shape, result.dtype)
        out_spec = pl.BlockSpec((share, tile), lambda f, c, info: (info[0], f))
    else:
        out_shape = jax.ShapeDtypeStruct((units, share), jnp.float32)
        out_spec = pl.BlockSpec((tile, share), lambda f, c, info: (f, 0))
    return pl.pallas_call(
        functools.partial(
            product_kernel, npieces, nsrc, acc_in is not None, final is not None, first, shares
        ),
        grid_spec=pltpu.PrefetchScalarGridSpec(
            num_scalar_prefetch=1,
            grid=(units // tile, npieces),
            in_specs=specs,
            out_specs=out_spec,
            scratch_shapes=[
                pltpu.VMEM((RING, tile, width), jnp.bfloat16),
                pltpu.VMEM((npieces, share, width), jnp.bfloat16),
                pltpu.VMEM((npieces, width, share), jnp.bfloat16),
                pltpu.VMEM((tile, share), jnp.float32),
                pltpu.SemaphoreType.DMA((npieces,)),
                pltpu.SemaphoreType.DMA((RING,)),
            ],
        ),
        out_shape=out_shape,
        input_output_aliases=aliases,
        compiler_params=pltpu.CompilerParams(
            dimension_semantics=("arbitrary", "arbitrary"), vmem_limit_bytes=VMEM_BYTES
        ),
        cost_estimate=pl.CostEstimate(
            flops=2 * share * width * npieces * units,
            bytes_accessed=2 * units * width * npieces,
            transcendentals=0,
        ),
        name="shard_product",
    )(info, *args)


def finish_kernel(info, *refs):
    acc0, acc1, s0, s1, a00, a01, a10, a11, out_ref = refs
    step = pl.program_id(0)
    for k, (acc, s_ref, factors) in enumerate(((acc0, s0, (a00, a01)), (acc1, s1, (a10, a11)))):

        @pl.when(step == k)
        def _():
            finish_rows(acc, s_ref, factors, (info[k, 4], info[k, 5]), out_ref)


def finish_two(info, acc0, acc1, scaled, factor, rows_total, tile):
    units, share = acc0.shape
    rank = scaled.shape[1]
    tiles = units // tile

    def acc_map(k):
        hold = tiles - 1 if k == 0 else 0
        return lambda s, f, info: (jnp.where(s == k, f, hold), 0)

    def factor_map(k, b):
        hold = tiles - 1 if k == 0 else 0
        return lambda s, f, info: (info[k, 2 + b], 0, jnp.where(s == k, f, hold))

    return pl.pallas_call(
        finish_kernel,
        grid_spec=pltpu.PrefetchScalarGridSpec(
            num_scalar_prefetch=1,
            grid=(2, tiles),
            in_specs=[
                pl.BlockSpec((tile, share), acc_map(0)),
                pl.BlockSpec((tile, share), acc_map(1)),
                pl.BlockSpec((SHARD_BLOCKS, rank, BLK), lambda s, f, info: (info[0, 0], 0, 0)),
                pl.BlockSpec((SHARD_BLOCKS, rank, BLK), lambda s, f, info: (info[1, 0], 0, 0)),
                pl.BlockSpec((1, rank, tile), factor_map(0, 0)),
                pl.BlockSpec((1, rank, tile), factor_map(0, 1)),
                pl.BlockSpec((1, rank, tile), factor_map(1, 0)),
                pl.BlockSpec((1, rank, tile), factor_map(1, 1)),
            ],
            out_specs=pl.BlockSpec((share, tile), lambda s, f, info: (info[s, 0], f)),
        ),
        out_shape=jax.ShapeDtypeStruct((rows_total, units), jnp.bfloat16),
        compiler_params=pltpu.CompilerParams(
            dimension_semantics=("arbitrary", "arbitrary"), vmem_limit_bytes=VMEM_BYTES
        ),
        cost_estimate=pl.CostEstimate(
            flops=4 * share * units * rank, bytes_accessed=12 * share * units, transcendentals=0
        ),
        name="finish_two",
    )(info, acc0, acc1, scaled, scaled, factor, factor, factor, factor)


def slice_kernel(n, tri, z_ref, adapters, slots, *refs):
    count = len(tri)
    own = refs[0]
    down = refs[1 : 1 + count]
    up = refs[1 + count : 1 + 2 * count]
    u_ref, s_ref, part_ref, grad_ref, rows_ref, sems = refs[1 + 2 * count :]
    share = rows_ref.shape[0] // n
    width = rows_ref.shape[1]
    z = z_ref[0]

    def each(do):
        for i, (j, c) in enumerate(tri):

            @pl.when(z == c)
            def _():
                do(pltpu.make_async_copy(
                    down[i], rows_ref.at[pl.ds((c + j) * share, share), :], sems.at[j]))

            @pl.when(z == n - 1 - c)
            def _():
                do(pltpu.make_async_copy(
                    up[i], rows_ref.at[pl.ds((n - 1 - c - j) * share, share), :], sems.at[n - 1 + j]))

    def own_copy():
        return pltpu.make_async_copy(
            own.at[:, pl.ds(pl.multiple_of(z * width, width), width)],
            rows_ref.at[pl.ds(pl.multiple_of(z * share, share), share), :],
            sems.at[0],
        )

    own_copy().start()
    each(lambda copy: copy.start())
    own_copy().wait()
    each(lambda copy: copy.wait())
    grad_ref[...] = jnp.zeros_like(grad_ref)
    for b in range(rows_ref.shape[0] // BLK):
        rows = slice(b * BLK, (b + 1) * BLK)
        dy = rows_ref[rows, :]
        part_ref[b] = lax.dot_general(
            dy, u_ref[adapters[b]], NT, preferred_element_type=jnp.float32
        ).T
        grad_ref[slots[b]] += (1.0 / BLK) * jnp.dot(
            s_ref[b], dy, preferred_element_type=jnp.float32
        )


def slice_terms(z, adapters, slots, own, down, up, factor, scaled_in, n, tri):
    count_adapters, rank, width = factor.shape
    total = scaled_in.shape[0] * BLK
    anyspec = pl.BlockSpec(memory_space=pltpu.HBM)
    vmem = pl.BlockSpec(memory_space=pltpu.VMEM)
    return pl.pallas_call(
        functools.partial(slice_kernel, n, tri),
        grid_spec=pltpu.PrefetchScalarGridSpec(
            num_scalar_prefetch=3,
            grid=(),
            in_specs=[anyspec] * (1 + 2 * len(tri)) + [vmem, vmem],
            out_specs=[vmem, vmem],
            scratch_shapes=[
                pltpu.VMEM((total, width), jnp.bfloat16),
                pltpu.SemaphoreType.DMA((2 * n - 1,)),
            ],
        ),
        out_shape=[
            jax.ShapeDtypeStruct(scaled_in.shape, jnp.float32),
            jax.ShapeDtypeStruct((count_adapters, rank, width), jnp.float32),
        ],
        compiler_params=pltpu.CompilerParams(vmem_limit_bytes=VMEM_BYTES),
        cost_estimate=pl.CostEstimate(
            flops=4 * total * width * rank,
            bytes_accessed=2 * total * width + 6 * count_adapters * rank * width,
            transcendentals=0,
        ),
        name="slice_terms",
    )(z, adapters, slots, own, *down, *up, factor, scaled_in)


def down_kernel(slots, s_ref, x_ref, grad_ref):
    grad_ref[...] = jnp.zeros_like(grad_ref)
    for b in range(x_ref.shape[0] // BLK):
        rows = slice(b * BLK, (b + 1) * BLK)
        grad_ref[slots[b]] += (1.0 / BLK) * jnp.dot(
            s_ref[b], x_ref[rows, :], preferred_element_type=jnp.float32
        )


def down_terms(slots, scaled_out, inputs, count_adapters, tile):
    total, units = inputs.shape
    rank = scaled_out.shape[1]
    return pl.pallas_call(
        down_kernel,
        grid_spec=pltpu.PrefetchScalarGridSpec(
            num_scalar_prefetch=1,
            grid=(units // tile,),
            in_specs=[
                pl.BlockSpec(scaled_out.shape, lambda f, slots: (0, 0, 0)),
                pl.BlockSpec((total, tile), lambda f, slots: (0, f)),
            ],
            out_specs=pl.BlockSpec((count_adapters, rank, tile), lambda f, slots: (0, 0, f)),
        ),
        out_shape=jax.ShapeDtypeStruct((count_adapters, rank, units), jnp.float32),
        compiler_params=pltpu.CompilerParams(
            dimension_semantics=("arbitrary",), vmem_limit_bytes=VMEM_BYTES
        ),
        cost_estimate=pl.CostEstimate(
            flops=2 * total * units * rank,
            bytes_accessed=2 * total * units + 4 * count_adapters * rank * units,
            transcendentals=0,
        ),
        name="down_terms",
    )(slots, scaled_out, inputs)


def on_line(
    upstream,
    hidden,
    frozen_weight,
    adapter_down_factor,
    adapter_up_factor,
    live_row_counts,
    adapter_of_block,
    gradient_owner_group,
):
    n = SHARES
    z = lax.axis_index("tp")
    own = upstream[0]
    share, features = own.shape
    width = features // n
    total = share * n
    units = hidden.shape[2]
    adapters = gradient_owner_group.shape[0]

    token_blocks = adapter_of_block[0]
    counts = live_counts(token_blocks, live_row_counts[0])
    slots = block_slots(token_blocks, gradient_owner_group)
    live = jnp.arange(BLK, dtype=jnp.int32)[None, None, :] < counts[:, None, None]
    inputs = hidden[0]

    def info_of(shard, candidate):
        pair = shard * SHARD_BLOCKS + jnp.arange(SHARD_BLOCKS, dtype=jnp.int32)
        hits = pair[:, None] == jnp.arange(token_blocks.shape[0], dtype=jnp.int32)[None, :]
        names = jnp.sum(jnp.where(hits, token_blocks[None, :], 0), axis=1)
        lives = jnp.sum(jnp.where(hits, counts[None, :], 0), axis=1)
        head = jnp.stack([shard, candidate]).astype(jnp.int32)
        return jnp.concatenate([head, names, lives])

    infos = [info_of(z, jnp.zeros((), jnp.int32))]
    for k in range(1, n):
        step_up = jnp.maximum(k - (n - 1 - z), 0)
        infos.append(info_of(jnp.where(step_up == 0, z + k, z - step_up), step_up))

    def held(value, *after):
        return lax.optimization_barrier((value, after))[0] if after else value

    def line_sum(terms):
        for distance in (1, 2):
            pairs = [(s, s ^ distance) for s in range(n)]
            terms = terms + lax.ppermute(terms, "tp", pairs)
        return terms

    down_factor_block = adapter_down_factor[token_blocks]
    inner = held(own[:, width:-width], down_factor_block)
    down = [[own[:, :width]]]
    down[0] += [inner[:, c * width : (c + 1) * width] for c in range(n - 2)]
    down[0] += [own[:, -width:]]
    up = [[down[0][n - 1 - c] for c in range(n)]]
    down += [[None] * n for _ in range(1, n)]
    up += [[None] * n for _ in range(1, n)]

    def send(place, *after):
        j, c = place
        to_lower = [(s, s - 1) for s in range(1, n) if s + j - 1 < n]
        to_upper = [(s, s + 1) for s in range(n - 1) if s - j + 1 >= 0]
        low, high = held((down[j - 1][c], up[j - 1][c]), *after)
        down[j][c] = lax.ppermute(low, "tp", to_lower)
        up[j][c] = lax.ppermute(high, "tp", to_upper)

    def came(place):
        j, c = place
        return (down[j][c], up[j][c])

    def candidates(k, lo, hi):
        return [down[k][lo:hi]] + [up[j][lo:hi] for j in range(1, k + 1)]

    order = [
        (1, 0), (1, 1), (2, 0), (1, 2), (2, 1), (3, 0),
        (1, 3), (2, 2), (3, 1), (2, 3), (3, 2), (3, 3),
    ]
    tri = [(j, c) for j in range(1, n) for c in range(n - j)]
    tile = 1024

    send(order[0])
    part_in = jnp.einsum(
        "bif,brf->bri",
        inputs.reshape(-1, BLK, units),
        down_factor_block,
        preferred_element_type=jnp.float32,
    )
    low_in = line_sum(part_in)
    send(order[1], part_in)
    send(order[2], came(order[0]))
    acc_own = shard_product(
        held(infos[0], came(order[0])), [down[0]], frozen_weight, 0, n, tile
    )
    send(order[3], came(order[1]), acc_own)
    send(order[4], came(order[2]))
    scaled_in = jnp.where(live, adapter_scale * low_in, 0.0).astype(jnp.bfloat16)
    send(order[5], came(order[3]), scaled_in)
    send(order[6], came(order[4]))
    send(order[7], came(order[5]))
    part_out, slot_up = slice_terms(
        z.reshape(1).astype(jnp.int32), token_blocks, slots, own,
        [down[j][c] for j, c in tri], [up[j][c] for j, c in tri],
        adapter_up_factor, scaled_in, n, tri,
    )
    low_out = line_sum(part_out)
    send(order[8], came(order[6]), part_out)
    acc_one = shard_product(
        held(infos[1], came(order[6]), part_out), candidates(1, 0, n), frozen_weight, 0, n, tile
    )
    grad_up = lax.psum_scatter(slot_up, "dp", scatter_dimension=0, tiled=True)
    send(order[9], came(order[7]), acc_one)
    send(order[10], came(order[8]))
    low_out = held(low_out, came(order[8]))
    scaled_out = jnp.where(live, adapter_scale * low_out, 0.0).astype(jnp.bfloat16)
    slot_down = down_terms(slots, scaled_out, inputs, adapters, 1024)
    grad_down = lax.psum_scatter(slot_down, "dp", scatter_dimension=0, tiled=True)
    result = finish_two(
        jnp.stack(infos[:2]), acc_own, acc_one, scaled_out, adapter_down_factor, total, tile
    )
    send(order[11], came(order[9]), result)
    result = shard_product(
        infos[2], candidates(2, 0, n), frozen_weight, 0, n, tile,
        final=(scaled_out, adapter_down_factor, result),
    )
    acc_last = shard_product(infos[3], candidates(3, 0, n - 1), frozen_weight, 0, n, tile)
    result = shard_product(
        infos[3], candidates(3, n - 1, n), frozen_weight, n - 1, n, tile, acc_in=acc_last,
        final=(scaled_out, adapter_down_factor, result),
    )
    return (result[None], grad_down, grad_up)


def gathered(
    upstream,
    hidden,
    frozen_weight,
    adapter_down_factor,
    adapter_up_factor,
    live_row_counts,
    adapter_of_block,
    gradient_owner_group,
):
    token_blocks = adapter_of_block[0]
    counts = live_counts(token_blocks, live_row_counts[0])
    slots = block_slots(token_blocks, gradient_owner_group)
    live = jnp.arange(BLK, dtype=jnp.int32)[None, :, None] < counts[:, None, None]
    inputs = hidden[0].reshape(-1, BLK, hidden.shape[2])
    down_factor = adapter_down_factor[token_blocks]
    local = adapter_up_factor.shape[2]
    grad_rows = lax.all_gather(upstream[0], "tp", axis=0, tiled=True)
    grad_slice = lax.dynamic_slice_in_dim(grad_rows, lax.axis_index("tp") * local, local, 1)
    grad_blk = grad_slice.reshape(-1, BLK, local)
    dot = functools.partial(jnp.einsum, preferred_element_type=jnp.float32)
    low_in, low_out = lax.psum(
        (
            dot("bif,brf->bir", inputs, down_factor),
            dot("bik,brk->bir", grad_blk, adapter_up_factor[token_blocks]),
        ),
        "tp",
    )
    scaled_in = jnp.where(live, adapter_scale * low_in, 0.0).astype(jnp.bfloat16)
    scaled_out = jnp.where(live, adapter_scale * low_out, 0.0).astype(jnp.bfloat16)
    base = lax.dot_general(grad_rows, frozen_weight, NT, preferred_element_type=jnp.float32)
    extra = dot("bir,brf->bif", scaled_out, down_factor)
    result = jnp.where(live, base.reshape(extra.shape) + extra, 0.0).astype(jnp.bfloat16)
    names = jnp.arange(gradient_owner_group.shape[0], dtype=jnp.int32)
    select = (names[:, None] == slots[None, :]).astype(jnp.float32)
    exact = functools.partial(jnp.einsum, precision=lax.Precision.HIGHEST)
    slot_down = exact("sb,brf->srf", select, dot("bir,bif->brf", scaled_out, inputs))
    slot_up = exact("sb,brk->srk", select, dot("bir,bik->brk", scaled_in, grad_blk))
    owned_down = lax.psum_scatter(slot_down, "dp", scatter_dimension=0, tiled=True)
    owned_up = lax.psum_scatter(slot_up, "dp", scatter_dimension=0, tiled=True)
    result = result.reshape(1, grad_rows.shape[0], -1)
    return (result, owned_down * (1.0 / BLK), owned_up * (1.0 / BLK))


def solution(mesh):
    return jax.shard_map(
        on_line if mesh.shape["tp"] == SHARES else gathered,
        mesh=mesh,
        in_specs=(
            P(("rep", "dp"), "tp", None),
            P(("rep", "dp"), None, "tp"),
            P("tp", None),
            P("rep", None, "tp"),
            P("rep", None, "tp"),
            P(("rep", "dp"), None),
            P(("rep", "dp"), None),
            P("rep"),
        ),
        out_specs=(
            P(("rep", "dp"), None, "tp"),
            P(("rep", "dp"), None, "tp"),
            P(("rep", "dp"), None, "tp"),
        ),
        check_vma=False,
    )
```

```python
import functools

import jax
import jax.numpy as jnp
from jax import lax
from jax.experimental import pallas as pl
from jax.experimental.pallas import tpu as pltpu
from jax.sharding import PartitionSpec as P

BLK = 128
SHARD_BLOCKS = 2
SHARES = 4
VMEM_BYTES = 60 << 20
RING = 4
LIGHT = pl.CostEstimate(flops=1024, bytes_accessed=1024, transcendentals=0)
LONG = pl.CostEstimate(flops=1 << 37, bytes_accessed=1 << 28, transcendentals=0)

adapter_scale = 2.0
NT = (((1,), (1,)), ((), ()))
TN = (((0,), (0,)), ((), ()))


def live_counts(token_blocks, counts):
    count_blocks = token_blocks.shape[0]
    same = token_blocks[:, None] == token_blocks[None, :]
    earlier = (
        jnp.arange(count_blocks, dtype=jnp.int32)[None, :]
        < jnp.arange(count_blocks, dtype=jnp.int32)[:, None]
    )
    ordinal = jnp.sum((same & earlier).astype(jnp.int32), axis=1)
    hits = token_blocks[:, None] == jnp.arange(counts.shape[0], dtype=jnp.int32)[None, :]
    limit = jnp.sum(jnp.where(hits, counts[None, :], 0), axis=1)
    return jnp.clip(limit - ordinal * BLK, 0, BLK)


def block_slots(token_blocks, owner):
    adapters = owner.shape[0]
    key = owner * adapters + jnp.arange(adapters, dtype=jnp.int32)
    slot = jnp.sum((key[None, :] < key[:, None]).astype(jnp.int32), axis=1)
    hits = token_blocks[:, None] == jnp.arange(adapters, dtype=jnp.int32)[None, :]
    return jnp.sum(jnp.where(hits, slot[None, :], 0), axis=1)


def product_kernel(table, npieces, nrefs, has_acc, final, first, shares, info, *refs):
    sources = refs[:nrefs]
    rest = list(refs[nrefs:])
    w_ref = rest.pop(0)
    acc_in = rest.pop(0) if has_acc else None
    if final:
        s_ref, a0_ref, a1_ref, _ = rest[:4]
        rest = rest[4:]
    out_ref, weights, lhs, turned, acc, sems, weight_sems = rest
    f, c = pl.program_id(0), pl.program_id(1)
    last = npieces - 1
    ring, tile, width = weights.shape
    step = f * npieces + c
    steps = pl.num_programs(0) * npieces

    def weight_copy(t):
        k = first + lax.rem(t, npieces)
        column = jnp.where(info[1] == 0, k, shares - 1 - k) * width
        block = w_ref.at[
            pl.ds(pl.multiple_of(lax.div(t, npieces) * tile, tile), tile),
            pl.ds(pl.multiple_of(column, width), width),
        ]
        slot = lax.rem(t, ring)
        return pltpu.make_async_copy(block, weights.at[slot], weight_sems.at[slot])

    @pl.when(step == 0)
    def _():
        for i, places in enumerate(table):

            @pl.when(info[1] == i)
            def _():
                for k, (which, column) in enumerate(places):
                    source = sources[which].at[:, column : column + width]
                    pltpu.make_async_copy(source, lhs.at[k], sems.at[k]).start()

        for t in range(ring):
            weight_copy(t).start()

    @pl.when((step > 0) & (step + ring - 1 < steps))
    def _():
        weight_copy(step + ring - 1).start()

    for k in range(npieces):

        @pl.when((f == 0) & (c == k))
        def _():
            which, column = table[0][k]
            source = sources[which].at[:, column : column + width]
            pltpu.make_async_copy(source, lhs.at[k], sems.at[k]).wait()
            turned[k] = lhs[k].T

    weight_copy(step).wait()
    part = jnp.dot(
        weights[lax.rem(step, ring)], turned[c], preferred_element_type=jnp.float32
    )

    @pl.when(c == 0)
    def _():
        acc[...] = part + acc_in[...] if has_acc else part

    @pl.when(c > 0)
    def _():
        acc[...] += part

    @pl.when(c == last)
    def _():
        if final:
            finish_rows(acc, s_ref, (a0_ref, a1_ref), (info[4], info[5]), out_ref)
        else:
            out_ref[...] = acc[...]


def finish_rows(acc, s_ref, factors, lives, out_ref, turned=True):
    for b, a_ref in enumerate(factors):
        rows = slice(b * BLK, (b + 1) * BLK)
        extra = lax.dot_general(s_ref[b], a_ref[0], TN, preferred_element_type=jnp.float32)
        base = acc[:, rows].T if turned else acc[rows, :]
        live = lax.broadcasted_iota(jnp.int32, base.shape, 0) < lives[b]
        out_ref[rows, :] = jnp.where(live, base + extra, 0.0).astype(out_ref.dtype)


def shard_product(info, candidates, weight, first, npieces, shares, tile, acc_in=None, final=None, cost=LIGHT):
    width = weight.shape[1] // shares
    sources, table = [], []
    for i, pieces in enumerate(candidates):
        places = []
        for k in range(first, first + npieces):
            start = (k if i == 0 else shares - 1 - k) * width
            for begin, piece in pieces:
                if begin <= start < begin + piece.shape[1]:
                    known = [j for j, source in enumerate(sources) if source is piece]
                    if not known:
                        sources.append(piece)
                        known = [len(sources) - 1]
                    places.append((known[0], start - begin))
        table.append(places)
    share = sources[0].shape[0]
    units = weight.shape[0]

    anyspec = pl.BlockSpec(memory_space=pltpu.HBM)
    args = sources + [weight]
    specs = [anyspec] * (len(sources) + 1)
    if acc_in is not None:
        args.append(acc_in)
        specs.append(pl.BlockSpec((tile, share), lambda f, c, info: (f, 0)))
    aliases = {}
    if final is not None:
        scaled, factor, result = final
        rank = scaled.shape[1]
        aliases = {1 + len(args) + 3: 0}
        args += [scaled, factor, factor, result]
        specs += [
            pl.BlockSpec((SHARD_BLOCKS, rank, BLK), lambda f, c, info: (info[0], 0, 0)),
            pl.BlockSpec((1, rank, tile), lambda f, c, info: (info[2], 0, f)),
            pl.BlockSpec((1, rank, tile), lambda f, c, info: (info[3], 0, f)),
            anyspec,
        ]
        out_shape = jax.ShapeDtypeStruct(result.shape, result.dtype)
        out_spec = pl.BlockSpec((share, tile), lambda f, c, info: (info[0], f))
    else:
        out_shape = jax.ShapeDtypeStruct((units, share), jnp.float32)
        out_spec = pl.BlockSpec((tile, share), lambda f, c, info: (f, 0))
    return pl.pallas_call(
        functools.partial(
            product_kernel, table, npieces, len(sources), acc_in is not None, final is not None,
            first, shares,
        ),
        grid_spec=pltpu.PrefetchScalarGridSpec(
            num_scalar_prefetch=1,
            grid=(units // tile, npieces),
            in_specs=specs,
            out_specs=out_spec,
            scratch_shapes=[
                pltpu.VMEM((RING, tile, width), jnp.bfloat16),
                pltpu.VMEM((npieces, share, width), jnp.bfloat16),
                pltpu.VMEM((npieces, width, share), jnp.bfloat16),
                pltpu.VMEM((tile, share), jnp.float32),
                pltpu.SemaphoreType.DMA((npieces,)),
                pltpu.SemaphoreType.DMA((RING,)),
            ],
        ),
        out_shape=out_shape,
        input_output_aliases=aliases,
        compiler_params=pltpu.CompilerParams(
            dimension_semantics=("arbitrary", "arbitrary"), vmem_limit_bytes=VMEM_BYTES
        ),
        cost_estimate=cost,
        name="shard_product",
    )(info, *args)


def finish_kernel(info, *refs):
    acc0, acc1, s0, s1, a00, a01, a10, a11, out_ref = refs
    step = pl.program_id(0)
    for k, (acc, s_ref, factors) in enumerate(((acc0, s0, (a00, a01)), (acc1, s1, (a10, a11)))):

        @pl.when(step == k)
        def _():
            finish_rows(acc, s_ref, factors, (info[k, 4], info[k, 5]), out_ref, turned=k == 1)


def finish_two(info, acc0, acc1, scaled, factor, rows_total, tile):
    share, units = acc0.shape
    rank = scaled.shape[1]
    tiles = units // tile

    def acc_map(k):
        if k == 0:
            return lambda s, f, info: (0, jnp.where(s == 0, f, tiles - 1))
        return lambda s, f, info: (jnp.where(s == 1, f, 0), 0)

    def factor_map(k, b):
        hold = tiles - 1 if k == 0 else 0
        return lambda s, f, info: (info[k, 2 + b], 0, jnp.where(s == k, f, hold))

    return pl.pallas_call(
        finish_kernel,
        grid_spec=pltpu.PrefetchScalarGridSpec(
            num_scalar_prefetch=1,
            grid=(2, tiles),
            in_specs=[
                pl.BlockSpec((share, tile), acc_map(0)),
                pl.BlockSpec((tile, share), acc_map(1)),
                pl.BlockSpec((SHARD_BLOCKS, rank, BLK), lambda s, f, info: (info[0, 0], 0, 0)),
                pl.BlockSpec((SHARD_BLOCKS, rank, BLK), lambda s, f, info: (info[1, 0], 0, 0)),
                pl.BlockSpec((1, rank, tile), factor_map(0, 0)),
                pl.BlockSpec((1, rank, tile), factor_map(0, 1)),
                pl.BlockSpec((1, rank, tile), factor_map(1, 0)),
                pl.BlockSpec((1, rank, tile), factor_map(1, 1)),
            ],
            out_specs=pl.BlockSpec((share, tile), lambda s, f, info: (info[s, 0], f)),
        ),
        out_shape=jax.ShapeDtypeStruct((rows_total, units), jnp.bfloat16),
        compiler_params=pltpu.CompilerParams(
            dimension_semantics=("arbitrary", "arbitrary"), vmem_limit_bytes=VMEM_BYTES
        ),
        cost_estimate=LIGHT,
        name="finish_two",
    )(info, acc0, acc1, scaled, scaled, factor, factor, factor, factor)


def cut_kernel(spans, rows_ref, *refs):
    sems = refs[-1]
    copies = [
        pltpu.make_async_copy(rows_ref.at[:, begin:end], refs[i], sems.at[i])
        for i, (begin, end) in enumerate(spans)
    ]
    for copy in copies:
        copy.start()
    for copy in copies:
        copy.wait()


def cut(rows, *spans):
    share = rows.shape[0]
    hbm = pl.BlockSpec(memory_space=pltpu.HBM)
    return pl.pallas_call(
        functools.partial(cut_kernel, spans),
        in_specs=[hbm],
        out_specs=[hbm] * len(spans),
        out_shape=[jax.ShapeDtypeStruct((share, end - begin), rows.dtype) for begin, end in spans],
        scratch_shapes=[pltpu.SemaphoreType.DMA((len(spans),))],
        compiler_params=pltpu.CompilerParams(vmem_limit_bytes=VMEM_BYTES),
        cost_estimate=LIGHT,
        name="cut",
    )(rows)


def slice_kernel(n, table, nrefs, z_ref, adapters, slots, *refs):
    own, sources = refs[0], refs[1 : 1 + nrefs]
    u_ref, s_ref, part_ref, grad_ref, rows_ref, sems = refs[1 + nrefs :]
    share = rows_ref.shape[0] // n
    width = rows_ref.shape[1]
    z = z_ref[0]

    def each(do):
        for i, (me, shard, which, column) in enumerate(table):

            @pl.when(z == me)
            def _():
                do(pltpu.make_async_copy(
                    sources[which].at[:, column : column + width],
                    rows_ref.at[shard * share : (shard + 1) * share, :],
                    sems.at[shard],
                ))

    def own_copy():
        return pltpu.make_async_copy(
            own.at[:, pl.ds(pl.multiple_of(z * width, width), width)],
            rows_ref.at[pl.ds(pl.multiple_of(z * share, share), share), :],
            sems.at[n],
        )

    own_copy().start()
    each(lambda copy: copy.start())
    own_copy().wait()
    each(lambda copy: copy.wait())
    grad_ref[...] = jnp.zeros_like(grad_ref)
    for b in range(rows_ref.shape[0] // BLK):
        rows = slice(b * BLK, (b + 1) * BLK)
        dy = rows_ref[rows, :]
        part_ref[b] = lax.dot_general(
            dy, u_ref[adapters[b]], NT, preferred_element_type=jnp.float32
        ).T
        grad_ref[slots[b]] += (1.0 / BLK) * jnp.dot(
            s_ref[b], dy, preferred_element_type=jnp.float32
        )


def slice_terms(z, adapters, slots, own, down, up, factor, scaled_in, n):
    count_adapters, rank, width = factor.shape
    total = scaled_in.shape[0] * BLK
    sources, table = [], []
    for me in range(n):
        for shard in range(n):
            if shard == me:
                continue
            for begin, piece in down[shard - me] if shard > me else up[me - shard]:
                if begin <= me * width < begin + piece.shape[1]:
                    known = [j for j, source in enumerate(sources) if source is piece]
                    if not known:
                        sources.append(piece)
                        known = [len(sources) - 1]
                    table.append((me, shard, known[0], me * width - begin))
    anyspec = pl.BlockSpec(memory_space=pltpu.HBM)
    vmem = pl.BlockSpec(memory_space=pltpu.VMEM)
    return pl.pallas_call(
        functools.partial(slice_kernel, n, table, len(sources)),
        grid_spec=pltpu.PrefetchScalarGridSpec(
            num_scalar_prefetch=3,
            grid=(),
            in_specs=[anyspec] * (1 + len(sources)) + [vmem, vmem],
            out_specs=[vmem, vmem],
            scratch_shapes=[
                pltpu.VMEM((total, width), jnp.bfloat16),
                pltpu.SemaphoreType.DMA((n + 1,)),
            ],
        ),
        out_shape=[
            jax.ShapeDtypeStruct(scaled_in.shape, jnp.float32),
            jax.ShapeDtypeStruct((count_adapters, rank, width), jnp.float32),
        ],
        compiler_params=pltpu.CompilerParams(vmem_limit_bytes=VMEM_BYTES),
        cost_estimate=LIGHT,
        name="slice_terms",
    )(z, adapters, slots, own, *sources, factor, scaled_in)


def down_kernel(slots, s_ref, x_ref, grad_ref):
    grad_ref[...] = jnp.zeros_like(grad_ref)
    for b in range(x_ref.shape[0] // BLK):
        rows = slice(b * BLK, (b + 1) * BLK)
        grad_ref[slots[b]] += (1.0 / BLK) * jnp.dot(
            s_ref[b], x_ref[rows, :], preferred_element_type=jnp.float32
        )


def down_terms(slots, scaled_out, inputs, count_adapters, tile):
    total, units = inputs.shape
    rank = scaled_out.shape[1]
    return pl.pallas_call(
        down_kernel,
        grid_spec=pltpu.PrefetchScalarGridSpec(
            num_scalar_prefetch=1,
            grid=(units // tile,),
            in_specs=[
                pl.BlockSpec(scaled_out.shape, lambda f, slots: (0, 0, 0)),
                pl.BlockSpec((total, tile), lambda f, slots: (0, f)),
            ],
            out_specs=pl.BlockSpec((count_adapters, rank, tile), lambda f, slots: (0, 0, f)),
        ),
        out_shape=jax.ShapeDtypeStruct((count_adapters, rank, units), jnp.float32),
        compiler_params=pltpu.CompilerParams(
            dimension_semantics=("arbitrary",), vmem_limit_bytes=VMEM_BYTES
        ),
        cost_estimate=LONG,
        name="down_terms",
    )(slots, scaled_out, inputs)


def on_line(
    upstream,
    hidden,
    frozen_weight,
    adapter_down_factor,
    adapter_up_factor,
    live_row_counts,
    adapter_of_block,
    gradient_owner_group,
):
    n = SHARES
    z = lax.axis_index("tp")
    own = upstream[0]
    share, features = own.shape
    width = features // n
    total = share * n
    units = hidden.shape[2]
    adapters = gradient_owner_group.shape[0]

    token_blocks = adapter_of_block[0]
    counts = live_counts(token_blocks, live_row_counts[0])
    slots = block_slots(token_blocks, gradient_owner_group)
    live = jnp.arange(BLK, dtype=jnp.int32)[None, None, :] < counts[:, None, None]
    inputs = hidden[0]

    def info_of(shard, candidate):
        pair = shard * SHARD_BLOCKS + jnp.arange(SHARD_BLOCKS, dtype=jnp.int32)
        hits = pair[:, None] == jnp.arange(token_blocks.shape[0], dtype=jnp.int32)[None, :]
        names = jnp.sum(jnp.where(hits, token_blocks[None, :], 0), axis=1)
        lives = jnp.sum(jnp.where(hits, counts[None, :], 0), axis=1)
        head = jnp.stack([shard, candidate]).astype(jnp.int32)
        return jnp.concatenate([head, names, lives])

    lower = (z >= n // 2).astype(jnp.int32)
    top = (z == n - 1).astype(jnp.int32)
    infos = [
        info_of(z, jnp.zeros((), jnp.int32)),
        info_of(jnp.where(top == 1, z - 1, z + 1), top),
        info_of(jnp.where(lower == 1, z - 2, z + 2), lower),
        info_of(
            jnp.where(z == 0, n - 1, jnp.where(top == 1, 0, z - 1)), jnp.minimum(z, 1) + top
        ),
    ]

    def held(value, *after):
        return lax.optimization_barrier((value, after))[0] if after else value

    def pair_sum(terms, distance, *after):
        pairs = [(s, s ^ distance) for s in range(n)]
        return held(terms + lax.ppermute(terms, "tp", pairs), *after)

    one_down = [(s, s - 1) for s in range(1, n)]
    one_up = [(s, s + 1) for s in range(n - 1)]
    two_down = [(s, s - 1) for s in range(1, n - 1)]
    two_up = [(s, s + 1) for s in range(1, n - 1)]
    far_down, far_up = [(n - 1, 0)], [(0, n - 1)]

    def move(pieces, pairs, *after):
        return [(begin, lax.ppermute(held(piece, *after), "tp", pairs)) for begin, piece in pieces]

    tile = 1024
    half = features // 2
    low, high = cut(own, (0, half), (half, features))
    near_d = move([(0, low), (half, high)], one_down)
    near_u = move([(half, high), (0, low)], one_up)
    first, middle, last = cut(
        held(own, low), (0, width), (width, features - width), (features - width, features)
    )
    down_factor_block = adapter_down_factor[token_blocks]
    part_in = jnp.einsum(
        "bif,brf->bri",
        inputs.reshape(-1, BLK, units),
        down_factor_block,
        preferred_element_type=jnp.float32,
    )
    acc_own = lax.dot_general(
        held(own, part_in), frozen_weight, NT, preferred_element_type=jnp.float32
    )
    low_in = pair_sum(part_in, 1)
    far_d = move([(0, first)], far_down, near_d[0], near_u[0], acc_own)
    far_u = move([(features - width, last)], far_up, near_d[0], near_u[0], acc_own)
    phase = (near_d[1], near_u[1], far_d[0], far_u[0], low_in)
    two_d = move(near_d[:1], two_down, far_d[0], far_u[0], low_in)
    two_u = move(near_u[:1], two_up, far_d[0], far_u[0], low_in)
    low_in = pair_sum(held(low_in, far_d[0], far_u[0]), 2)
    two_d += move(near_d[1:], two_down, phase)
    two_u += move(near_u[1:], two_up, phase)
    acc_one = shard_product(
        held(infos[1], phase), [near_d, near_u], frozen_weight, 0, n, n, tile, cost=LONG
    )
    scaled_in = jnp.where(live, adapter_scale * low_in, 0.0).astype(jnp.bfloat16)
    part_out, slot_up = slice_terms(
        z.reshape(1).astype(jnp.int32), held(token_blocks, acc_one), slots, own,
        {1: near_d, 2: two_d[:1], 3: far_d}, {1: near_u, 2: two_u[:1], 3: far_u},
        adapter_up_factor, scaled_in, n,
    )
    grad_up = lax.psum_scatter(slot_up, "dp", scatter_dimension=0, tiled=True)
    low_out = pair_sum(part_out, 1)
    acc_two = shard_product(
        held(infos[2], part_out), [two_d[:1], two_u[:1]], frozen_weight, 0, n // 2, n, tile
    )
    phase = (two_d[1], two_u[1], acc_two)
    far_d += move([(width, middle), (features - width, last)], far_down, phase)
    far_u += move([(width, middle), (0, first)], far_up, phase)
    low_out = pair_sum(held(low_out, phase), 2)
    scaled_out = jnp.where(live, adapter_scale * low_out, 0.0).astype(jnp.bfloat16)
    result = finish_two(
        jnp.stack(infos[:2]), acc_own, acc_one, scaled_out, adapter_down_factor, total, tile
    )
    slot_down = down_terms(slots, held(scaled_out, result), inputs, adapters, 1024)
    grad_down = lax.psum_scatter(slot_down, "dp", scatter_dimension=0, tiled=True)
    result = shard_product(
        held(infos[2], slot_down), [two_d[1:], two_u[1:]], frozen_weight, n // 2, n // 2, n,
        tile, acc_in=acc_two, final=(scaled_out, adapter_down_factor, result),
    )
    acc_last = shard_product(
        held(infos[3], result), [far_d[:2], near_u, far_u[:2]], frozen_weight, 0, n - 1, n, tile
    )
    result = shard_product(
        infos[3], [far_d[2:], near_u, far_u[2:]], frozen_weight, n - 1, 1, n, tile,
        acc_in=acc_last, final=(scaled_out, adapter_down_factor, result),
    )
    return (result[None], grad_down, grad_up)


def gathered(
    upstream,
    hidden,
    frozen_weight,
    adapter_down_factor,
    adapter_up_factor,
    live_row_counts,
    adapter_of_block,
    gradient_owner_group,
):
    token_blocks = adapter_of_block[0]
    counts = live_counts(token_blocks, live_row_counts[0])
    slots = block_slots(token_blocks, gradient_owner_group)
    live = jnp.arange(BLK, dtype=jnp.int32)[None, :, None] < counts[:, None, None]
    inputs = hidden[0].reshape(-1, BLK, hidden.shape[2])
    down_factor = adapter_down_factor[token_blocks]
    local = adapter_up_factor.shape[2]
    grad_rows = lax.all_gather(upstream[0], "tp", axis=0, tiled=True)
    grad_slice = lax.dynamic_slice_in_dim(grad_rows, lax.axis_index("tp") * local, local, 1)
    grad_blk = grad_slice.reshape(-1, BLK, local)
    dot = functools.partial(jnp.einsum, preferred_element_type=jnp.float32)
    low_in, low_out = lax.psum(
        (
            dot("bif,brf->bir", inputs, down_factor),
            dot("bik,brk->bir", grad_blk, adapter_up_factor[token_blocks]),
        ),
        "tp",
    )
    scaled_in = jnp.where(live, adapter_scale * low_in, 0.0).astype(jnp.bfloat16)
    scaled_out = jnp.where(live, adapter_scale * low_out, 0.0).astype(jnp.bfloat16)
    base = lax.dot_general(grad_rows, frozen_weight, NT, preferred_element_type=jnp.float32)
    extra = dot("bir,brf->bif", scaled_out, down_factor)
    result = jnp.where(live, base.reshape(extra.shape) + extra, 0.0).astype(jnp.bfloat16)
    names = jnp.arange(gradient_owner_group.shape[0], dtype=jnp.int32)
    select = (names[:, None] == slots[None, :]).astype(jnp.float32)
    exact = functools.partial(jnp.einsum, precision=lax.Precision.HIGHEST)
    slot_down = exact("sb,brf->srf", select, dot("bir,bif->brf", scaled_out, inputs))
    slot_up = exact("sb,brk->srk", select, dot("bir,bik->brk", scaled_in, grad_blk))
    owned_down = lax.psum_scatter(slot_down, "dp", scatter_dimension=0, tiled=True)
    owned_up = lax.psum_scatter(slot_up, "dp", scatter_dimension=0, tiled=True)
    result = result.reshape(1, grad_rows.shape[0], -1)
    return (result, owned_down * (1.0 / BLK), owned_up * (1.0 / BLK))


def solution(mesh):
    return jax.shard_map(
        on_line if mesh.shape["tp"] == SHARES else gathered,
        mesh=mesh,
        in_specs=(
            P(("rep", "dp"), "tp", None),
            P(("rep", "dp"), None, "tp"),
            P("tp", None),
            P("rep", None, "tp"),
            P("rep", None, "tp"),
            P(("rep", "dp"), None),
            P(("rep", "dp"), None),
            P("rep"),
        ),
        out_specs=(
            P(("rep", "dp"), None, "tp"),
            P(("rep", "dp"), None, "tp"),
            P(("rep", "dp"), None, "tp"),
        ),
        check_vma=False,
    )
```

```python
import functools

import jax
import jax.numpy as jnp
from jax import lax
from jax.experimental import pallas as pl
from jax.experimental.pallas import tpu as pltpu
from jax.sharding import PartitionSpec as P

BLK = 128
SHARD_BLOCKS = 2
SHARES = 4
VMEM_BYTES = 60 << 20
RING = 4
LIGHT = pl.CostEstimate(flops=1024, bytes_accessed=1024, transcendentals=0)
LONG = pl.CostEstimate(flops=1 << 37, bytes_accessed=1 << 28, transcendentals=0)

adapter_scale = 2.0
NT = (((1,), (1,)), ((), ()))
TN = (((0,), (0,)), ((), ()))


def live_counts(token_blocks, counts):
    count_blocks = token_blocks.shape[0]
    same = token_blocks[:, None] == token_blocks[None, :]
    earlier = (
        jnp.arange(count_blocks, dtype=jnp.int32)[None, :]
        < jnp.arange(count_blocks, dtype=jnp.int32)[:, None]
    )
    ordinal = jnp.sum((same & earlier).astype(jnp.int32), axis=1)
    hits = token_blocks[:, None] == jnp.arange(counts.shape[0], dtype=jnp.int32)[None, :]
    limit = jnp.sum(jnp.where(hits, counts[None, :], 0), axis=1)
    return jnp.clip(limit - ordinal * BLK, 0, BLK)


def block_slots(token_blocks, owner):
    adapters = owner.shape[0]
    key = owner * adapters + jnp.arange(adapters, dtype=jnp.int32)
    slot = jnp.sum((key[None, :] < key[:, None]).astype(jnp.int32), axis=1)
    hits = token_blocks[:, None] == jnp.arange(adapters, dtype=jnp.int32)[None, :]
    return jnp.sum(jnp.where(hits, slot[None, :], 0), axis=1)


def product_kernel(table, npieces, nrefs, has_acc, final, first, shares, info, *refs):
    sources = refs[:nrefs]
    rest = list(refs[nrefs:])
    w_ref = rest.pop(0)
    acc_in = rest.pop(0) if has_acc else None
    if final:
        s_ref, a0_ref, a1_ref, _ = rest[:4]
        rest = rest[4:]
    out_ref, weights, lhs, turned, acc, sems, weight_sems = rest
    f, c = pl.program_id(0), pl.program_id(1)
    last = npieces - 1
    ring, tile, width = weights.shape
    step = f * npieces + c
    steps = pl.num_programs(0) * npieces

    def weight_copy(t):
        k = first + lax.rem(t, npieces)
        column = jnp.where(info[1] == 0, k, shares - 1 - k) * width
        block = w_ref.at[
            pl.ds(pl.multiple_of(lax.div(t, npieces) * tile, tile), tile),
            pl.ds(pl.multiple_of(column, width), width),
        ]
        slot = lax.rem(t, ring)
        return pltpu.make_async_copy(block, weights.at[slot], weight_sems.at[slot])

    @pl.when(step == 0)
    def _():
        for i, places in enumerate(table):

            @pl.when(info[1] == i)
            def _():
                for k, (which, column) in enumerate(places):
                    source = sources[which].at[:, column : column + width]
                    pltpu.make_async_copy(source, lhs.at[k], sems.at[k]).start()

        for t in range(ring):
            weight_copy(t).start()

    @pl.when((step > 0) & (step + ring - 1 < steps))
    def _():
        weight_copy(step + ring - 1).start()

    for k in range(npieces):

        @pl.when((f == 0) & (c == k))
        def _():
            which, column = table[0][k]
            source = sources[which].at[:, column : column + width]
            pltpu.make_async_copy(source, lhs.at[k], sems.at[k]).wait()
            turned[k] = lhs[k].T

    weight_copy(step).wait()
    part = jnp.dot(
        weights[lax.rem(step, ring)], turned[c], preferred_element_type=jnp.float32
    )

    @pl.when(c == 0)
    def _():
        acc[...] = part + acc_in[...] if has_acc else part

    @pl.when(c > 0)
    def _():
        acc[...] += part

    @pl.when(c == last)
    def _():
        if final:
            finish_rows(acc, s_ref, (a0_ref, a1_ref), (info[4], info[5]), out_ref)
        else:
            out_ref[...] = acc[...]


def finish_rows(acc, s_ref, factors, lives, out_ref, turned=True):
    for b, a_ref in enumerate(factors):
        rows = slice(b * BLK, (b + 1) * BLK)
        extra = lax.dot_general(s_ref[b], a_ref[0], TN, preferred_element_type=jnp.float32)
        base = acc[:, rows].T if turned else acc[rows, :]
        live = lax.broadcasted_iota(jnp.int32, base.shape, 0) < lives[b]
        out_ref[rows, :] = jnp.where(live, base + extra, 0.0).astype(out_ref.dtype)


def shard_product(info, candidates, weight, first, npieces, shares, tile, acc_in=None, final=None, cost=LIGHT):
    width = weight.shape[1] // shares
    sources, table = [], []
    for i, pieces in enumerate(candidates):
        places = []
        for k in range(first, first + npieces):
            start = (k if i == 0 else shares - 1 - k) * width
            for begin, piece in pieces:
                if begin <= start < begin + piece.shape[1]:
                    known = [j for j, source in enumerate(sources) if source is piece]
                    if not known:
                        sources.append(piece)
                        known = [len(sources) - 1]
                    places.append((known[0], start - begin))
        table.append(places)
    share = sources[0].shape[0]
    units = weight.shape[0]

    anyspec = pl.BlockSpec(memory_space=pltpu.HBM)
    args = sources + [weight]
    specs = [anyspec] * (len(sources) + 1)
    if acc_in is not None:
        args.append(acc_in)
        specs.append(pl.BlockSpec((tile, share), lambda f, c, info: (f, 0)))
    aliases = {}
    if final is not None:
        scaled, factor, result = final
        rank = scaled.shape[1]
        aliases = {1 + len(args) + 3: 0}
        args += [scaled, factor, factor, result]
        specs += [
            pl.BlockSpec((SHARD_BLOCKS, rank, BLK), lambda f, c, info: (info[0], 0, 0)),
            pl.BlockSpec((1, rank, tile), lambda f, c, info: (info[2], 0, f)),
            pl.BlockSpec((1, rank, tile), lambda f, c, info: (info[3], 0, f)),
            anyspec,
        ]
        out_shape = jax.ShapeDtypeStruct(result.shape, result.dtype)
        out_spec = pl.BlockSpec((share, tile), lambda f, c, info: (info[0], f))
    else:
        out_shape = jax.ShapeDtypeStruct((units, share), jnp.float32)
        out_spec = pl.BlockSpec((tile, share), lambda f, c, info: (f, 0))
    return pl.pallas_call(
        functools.partial(
            product_kernel, table, npieces, len(sources), acc_in is not None, final is not None,
            first, shares,
        ),
        grid_spec=pltpu.PrefetchScalarGridSpec(
            num_scalar_prefetch=1,
            grid=(units // tile, npieces),
            in_specs=specs,
            out_specs=out_spec,
            scratch_shapes=[
                pltpu.VMEM((RING, tile, width), jnp.bfloat16),
                pltpu.VMEM((npieces, share, width), jnp.bfloat16),
                pltpu.VMEM((npieces, width, share), jnp.bfloat16),
                pltpu.VMEM((tile, share), jnp.float32),
                pltpu.SemaphoreType.DMA((npieces,)),
                pltpu.SemaphoreType.DMA((RING,)),
            ],
        ),
        out_shape=out_shape,
        input_output_aliases=aliases,
        compiler_params=pltpu.CompilerParams(
            dimension_semantics=("arbitrary", "arbitrary"), vmem_limit_bytes=VMEM_BYTES
        ),
        cost_estimate=cost,
        name="shard_product",
    )(info, *args)


def finish_kernel(info, *refs):
    acc0, acc1, s0, s1, a00, a01, a10, a11, out_ref = refs
    step = pl.program_id(0)
    for k, (acc, s_ref, factors) in enumerate(((acc0, s0, (a00, a01)), (acc1, s1, (a10, a11)))):

        @pl.when(step == k)
        def _():
            finish_rows(acc, s_ref, factors, (info[k, 4], info[k, 5]), out_ref, turned=k == 1)


def finish_two(info, acc0, acc1, scaled, factor, rows_total, tile):
    share, units = acc0.shape
    rank = scaled.shape[1]
    tiles = units // tile

    def acc_map(k):
        if k == 0:
            return lambda s, f, info: (0, jnp.where(s == 0, f, tiles - 1))
        return lambda s, f, info: (jnp.where(s == 1, f, 0), 0)

    def factor_map(k, b):
        hold = tiles - 1 if k == 0 else 0
        return lambda s, f, info: (info[k, 2 + b], 0, jnp.where(s == k, f, hold))

    return pl.pallas_call(
        finish_kernel,
        grid_spec=pltpu.PrefetchScalarGridSpec(
            num_scalar_prefetch=1,
            grid=(2, tiles),
            in_specs=[
                pl.BlockSpec((share, tile), acc_map(0)),
                pl.BlockSpec((tile, share), acc_map(1)),
                pl.BlockSpec((SHARD_BLOCKS, rank, BLK), lambda s, f, info: (info[0, 0], 0, 0)),
                pl.BlockSpec((SHARD_BLOCKS, rank, BLK), lambda s, f, info: (info[1, 0], 0, 0)),
                pl.BlockSpec((1, rank, tile), factor_map(0, 0)),
                pl.BlockSpec((1, rank, tile), factor_map(0, 1)),
                pl.BlockSpec((1, rank, tile), factor_map(1, 0)),
                pl.BlockSpec((1, rank, tile), factor_map(1, 1)),
            ],
            out_specs=pl.BlockSpec((share, tile), lambda s, f, info: (info[s, 0], f)),
        ),
        out_shape=jax.ShapeDtypeStruct((rows_total, units), jnp.bfloat16),
        compiler_params=pltpu.CompilerParams(
            dimension_semantics=("arbitrary", "arbitrary"), vmem_limit_bytes=VMEM_BYTES
        ),
        cost_estimate=LIGHT,
        name="finish_two",
    )(info, acc0, acc1, scaled, scaled, factor, factor, factor, factor)


def slice_kernel(n, table, nrefs, z_ref, adapters, slots, *refs):
    own, sources = refs[0], refs[1 : 1 + nrefs]
    u_ref, s_ref, part_ref, grad_ref, rows_ref, sems = refs[1 + nrefs :]
    share = rows_ref.shape[0] // n
    width = rows_ref.shape[1]
    z = z_ref[0]

    def each(do):
        for i, (me, shard, which, column) in enumerate(table):

            @pl.when(z == me)
            def _():
                do(pltpu.make_async_copy(
                    sources[which].at[:, column : column + width],
                    rows_ref.at[shard * share : (shard + 1) * share, :],
                    sems.at[shard],
                ))

    def own_copy():
        return pltpu.make_async_copy(
            own.at[:, pl.ds(pl.multiple_of(z * width, width), width)],
            rows_ref.at[pl.ds(pl.multiple_of(z * share, share), share), :],
            sems.at[n],
        )

    own_copy().start()
    each(lambda copy: copy.start())
    own_copy().wait()
    each(lambda copy: copy.wait())
    grad_ref[...] = jnp.zeros_like(grad_ref)
    for b in range(rows_ref.shape[0] // BLK):
        rows = slice(b * BLK, (b + 1) * BLK)
        dy = rows_ref[rows, :]
        part_ref[b] = lax.dot_general(
            dy, u_ref[adapters[b]], NT, preferred_element_type=jnp.float32
        ).T
        grad_ref[slots[b]] += (1.0 / BLK) * jnp.dot(
            s_ref[b], dy, preferred_element_type=jnp.float32
        )


def slice_terms(z, adapters, slots, own, down, up, factor, scaled_in, n):
    count_adapters, rank, width = factor.shape
    total = scaled_in.shape[0] * BLK
    sources, table = [], []
    for me in range(n):
        for shard in range(n):
            if shard == me:
                continue
            for begin, piece in down[shard - me] if shard > me else up[me - shard]:
                if begin <= me * width < begin + piece.shape[1]:
                    known = [j for j, source in enumerate(sources) if source is piece]
                    if not known:
                        sources.append(piece)
                        known = [len(sources) - 1]
                    table.append((me, shard, known[0], me * width - begin))
    anyspec = pl.BlockSpec(memory_space=pltpu.HBM)
    vmem = pl.BlockSpec(memory_space=pltpu.VMEM)
    return pl.pallas_call(
        functools.partial(slice_kernel, n, table, len(sources)),
        grid_spec=pltpu.PrefetchScalarGridSpec(
            num_scalar_prefetch=3,
            grid=(),
            in_specs=[anyspec] * (1 + len(sources)) + [vmem, vmem],
            out_specs=[vmem, vmem],
            scratch_shapes=[
                pltpu.VMEM((total, width), jnp.bfloat16),
                pltpu.SemaphoreType.DMA((n + 1,)),
            ],
        ),
        out_shape=[
            jax.ShapeDtypeStruct(scaled_in.shape, jnp.float32),
            jax.ShapeDtypeStruct((count_adapters, rank, width), jnp.float32),
        ],
        compiler_params=pltpu.CompilerParams(vmem_limit_bytes=VMEM_BYTES),
        cost_estimate=LIGHT,
        name="slice_terms",
    )(z, adapters, slots, own, *sources, factor, scaled_in)


def down_kernel(slots, s_ref, x_ref, grad_ref):
    grad_ref[...] = jnp.zeros_like(grad_ref)
    for b in range(x_ref.shape[0] // BLK):
        rows = slice(b * BLK, (b + 1) * BLK)
        grad_ref[slots[b]] += (1.0 / BLK) * jnp.dot(
            s_ref[b], x_ref[rows, :], preferred_element_type=jnp.float32
        )


def down_terms(slots, scaled_out, inputs, count_adapters, tile):
    total, units = inputs.shape
    rank = scaled_out.shape[1]
    return pl.pallas_call(
        down_kernel,
        grid_spec=pltpu.PrefetchScalarGridSpec(
            num_scalar_prefetch=1,
            grid=(units // tile,),
            in_specs=[
                pl.BlockSpec(scaled_out.shape, lambda f, slots: (0, 0, 0)),
                pl.BlockSpec((total, tile), lambda f, slots: (0, f)),
            ],
            out_specs=pl.BlockSpec((count_adapters, rank, tile), lambda f, slots: (0, 0, f)),
        ),
        out_shape=jax.ShapeDtypeStruct((count_adapters, rank, units), jnp.float32),
        compiler_params=pltpu.CompilerParams(
            dimension_semantics=("arbitrary",), vmem_limit_bytes=VMEM_BYTES
        ),
        cost_estimate=LONG,
        name="down_terms",
    )(slots, scaled_out, inputs)


def on_line(
    upstream,
    hidden,
    frozen_weight,
    adapter_down_factor,
    adapter_up_factor,
    live_row_counts,
    adapter_of_block,
    gradient_owner_group,
):
    n = SHARES
    z = lax.axis_index("tp")
    own = upstream[0]
    share, features = own.shape
    width = features // n
    total = share * n
    units = hidden.shape[2]
    adapters = gradient_owner_group.shape[0]

    token_blocks = adapter_of_block[0]
    counts = live_counts(token_blocks, live_row_counts[0])
    slots = block_slots(token_blocks, gradient_owner_group)
    live = jnp.arange(BLK, dtype=jnp.int32)[None, None, :] < counts[:, None, None]
    inputs = hidden[0]

    def info_of(shard, candidate):
        pair = shard * SHARD_BLOCKS + jnp.arange(SHARD_BLOCKS, dtype=jnp.int32)
        hits = pair[:, None] == jnp.arange(token_blocks.shape[0], dtype=jnp.int32)[None, :]
        names = jnp.sum(jnp.where(hits, token_blocks[None, :], 0), axis=1)
        lives = jnp.sum(jnp.where(hits, counts[None, :], 0), axis=1)
        head = jnp.stack([shard, candidate]).astype(jnp.int32)
        return jnp.concatenate([head, names, lives])

    lower = (z >= n // 2).astype(jnp.int32)
    top = (z == n - 1).astype(jnp.int32)
    infos = [
        info_of(z, jnp.zeros((), jnp.int32)),
        info_of(jnp.where(top == 1, z - 1, z + 1), top),
        info_of(jnp.where(lower == 1, z - 2, z + 2), lower),
        info_of(
            jnp.where(z == 0, n - 1, jnp.where(top == 1, 0, z - 1)), jnp.minimum(z, 1) + top
        ),
    ]

    def held(value, *after):
        return lax.optimization_barrier((value, after))[0] if after else value

    def pair_sum(terms, distance, *after):
        pairs = [(s, s ^ distance) for s in range(n)]
        return held(terms + lax.ppermute(terms, "tp", pairs), *after)

    one_down = [(s, s - 1) for s in range(1, n)]
    one_up = [(s, s + 1) for s in range(n - 1)]
    two_down = [(s, s - 1) for s in range(1, n - 1)]
    two_up = [(s, s + 1) for s in range(1, n - 1)]
    far_down, far_up = [(n - 1, 0)], [(0, n - 1)]

    def move(pieces, pairs, *after):
        return [(begin, lax.ppermute(held(piece, *after), "tp", pairs)) for begin, piece in pieces]

    tile = 1024
    half = features // 2
    low, high = own[:, :half], own[:, half:]
    near_d = move([(0, low), (half, high)], one_down)
    near_u = move([(0, low), (half, high)], one_up)
    part_in = jnp.einsum(
        "bif,brf->bri",
        inputs.reshape(-1, BLK, units),
        adapter_down_factor[token_blocks],
        preferred_element_type=jnp.float32,
    )
    phase = (near_d[0], near_u[0])
    rest = held(own, part_in)
    first, middle, last = rest[:, :width], rest[:, width:-width], rest[:, -width:]
    far_d = move([(0, first)], far_down, phase)
    far_u = move([(features - width, last)], far_up, phase)
    corner = near_d[0][1][:8, :BLK]
    low_in = pair_sum(held(part_in, corner), 1)
    acc_own = lax.dot_general(
        held(own, corner), frozen_weight, NT, preferred_element_type=jnp.float32
    )
    low_in = pair_sum(held(low_in, acc_own), 2)
    phase = (near_d[1], near_u[1], far_d[0], far_u[0], low_in, acc_own)
    two_d = move(near_d[:1], two_down, phase)
    two_u = move(near_u[1:], two_up, phase)
    acc_one = shard_product(
        held(infos[1], phase), [near_d, near_u], frozen_weight, 0, n, n, tile, cost=LONG
    )
    two_d += move(near_d[1:], two_down, acc_one)
    two_u += move(near_u[:1], two_up, acc_one)
    phase = (two_d[0], two_u[0], acc_one)
    far_d += move([(width, middle)], far_down, phase)
    far_u += move([(width, middle)], far_up, phase)
    scaled_in = jnp.where(live, adapter_scale * held(low_in, phase), 0.0).astype(jnp.bfloat16)
    part_out, slot_up = slice_terms(
        z.reshape(1).astype(jnp.int32), held(token_blocks, phase), slots, own,
        {1: near_d, 2: two_d[:1], 3: far_d[:1]}, {1: near_u, 2: two_u[:1], 3: far_u[:1]},
        adapter_up_factor, scaled_in, n,
    )
    low_out = held(lax.psum(part_out, "tp"), two_d[1], two_u[1])
    grad_up = lax.psum_scatter(slot_up, "dp", scatter_dimension=0, tiled=True)
    scaled_out = jnp.where(live, adapter_scale * low_out, 0.0).astype(jnp.bfloat16)
    slot_down = down_terms(slots, scaled_out, inputs, adapters, 1024)
    grad_down = lax.psum_scatter(slot_down, "dp", scatter_dimension=0, tiled=True)
    result = finish_two(
        jnp.stack(infos[:2]), acc_own, acc_one, held(scaled_out, slot_down),
        adapter_down_factor, total, tile,
    )
    phase = (two_d[1], two_u[1], result)
    far_d += move([(features - width, last)], far_down, phase)
    far_u += move([(0, first)], far_up, phase)
    result = shard_product(
        held(infos[2], phase), [two_d, two_u], frozen_weight, 0, n, n,
        tile, final=(scaled_out, adapter_down_factor, result), cost=LONG,
    )
    acc_last = shard_product(
        held(infos[3], result), [far_d[:2], near_u, far_u[:2]], frozen_weight, 0, n - 1, n, tile
    )
    result = shard_product(
        infos[3], [far_d[2:], near_u, far_u[2:]], frozen_weight, n - 1, 1, n, tile,
        acc_in=acc_last, final=(scaled_out, adapter_down_factor, result),
    )
    return (result[None], grad_down, grad_up)


def gathered(
    upstream,
    hidden,
    frozen_weight,
    adapter_down_factor,
    adapter_up_factor,
    live_row_counts,
    adapter_of_block,
    gradient_owner_group,
):
    token_blocks = adapter_of_block[0]
    counts = live_counts(token_blocks, live_row_counts[0])
    slots = block_slots(token_blocks, gradient_owner_group)
    live = jnp.arange(BLK, dtype=jnp.int32)[None, :, None] < counts[:, None, None]
    inputs = hidden[0].reshape(-1, BLK, hidden.shape[2])
    down_factor = adapter_down_factor[token_blocks]
    local = adapter_up_factor.shape[2]
    grad_rows = lax.all_gather(upstream[0], "tp", axis=0, tiled=True)
    grad_slice = lax.dynamic_slice_in_dim(grad_rows, lax.axis_index("tp") * local, local, 1)
    grad_blk = grad_slice.reshape(-1, BLK, local)
    dot = functools.partial(jnp.einsum, preferred_element_type=jnp.float32)
    low_in, low_out = lax.psum(
        (
            dot("bif,brf->bir", inputs, down_factor),
            dot("bik,brk->bir", grad_blk, adapter_up_factor[token_blocks]),
        ),
        "tp",
    )
    scaled_in = jnp.where(live, adapter_scale * low_in, 0.0).astype(jnp.bfloat16)
    scaled_out = jnp.where(live, adapter_scale * low_out, 0.0).astype(jnp.bfloat16)
    base = lax.dot_general(grad_rows, frozen_weight, NT, preferred_element_type=jnp.float32)
    extra = dot("bir,brf->bif", scaled_out, down_factor)
    result = jnp.where(live, base.reshape(extra.shape) + extra, 0.0).astype(jnp.bfloat16)
    names = jnp.arange(gradient_owner_group.shape[0], dtype=jnp.int32)
    select = (names[:, None] == slots[None, :]).astype(jnp.float32)
    exact = functools.partial(jnp.einsum, precision=lax.Precision.HIGHEST)
    slot_down = exact("sb,brf->srf", select, dot("bir,bif->brf", scaled_out, inputs))
    slot_up = exact("sb,brk->srk", select, dot("bir,bik->brk", scaled_in, grad_blk))
    owned_down = lax.psum_scatter(slot_down, "dp", scatter_dimension=0, tiled=True)
    owned_up = lax.psum_scatter(slot_up, "dp", scatter_dimension=0, tiled=True)
    result = result.reshape(1, grad_rows.shape[0], -1)
    return (result, owned_down * (1.0 / BLK), owned_up * (1.0 / BLK))


def solution(mesh):
    return jax.shard_map(
        on_line if mesh.shape["tp"] == SHARES else gathered,
        mesh=mesh,
        in_specs=(
            P(("rep", "dp"), "tp", None),
            P(("rep", "dp"), None, "tp"),
            P("tp", None),
            P("rep", None, "tp"),
            P("rep", None, "tp"),
            P(("rep", "dp"), None),
            P(("rep", "dp"), None),
            P("rep"),
        ),
        out_specs=(
            P(("rep", "dp"), None, "tp"),
            P(("rep", "dp"), None, "tp"),
            P(("rep", "dp"), None, "tp"),
        ),
        check_vma=False,
    )
```

```python
import functools

import jax
import jax.numpy as jnp
from jax import lax
from jax.experimental import pallas as pl
from jax.experimental.pallas import tpu as pltpu
from jax.sharding import PartitionSpec as P

BLK = 128
SHARD_BLOCKS = 2
SHARES = 4
VMEM_BYTES = 60 << 20
RING = 4
LIGHT = pl.CostEstimate(flops=1024, bytes_accessed=1024, transcendentals=0)
LONG = pl.CostEstimate(flops=1 << 37, bytes_accessed=1 << 28, transcendentals=0)

adapter_scale = 2.0
NT = (((1,), (1,)), ((), ()))
TN = (((0,), (0,)), ((), ()))


def live_counts(token_blocks, counts):
    count_blocks = token_blocks.shape[0]
    same = token_blocks[:, None] == token_blocks[None, :]
    earlier = (
        jnp.arange(count_blocks, dtype=jnp.int32)[None, :]
        < jnp.arange(count_blocks, dtype=jnp.int32)[:, None]
    )
    ordinal = jnp.sum((same & earlier).astype(jnp.int32), axis=1)
    hits = token_blocks[:, None] == jnp.arange(counts.shape[0], dtype=jnp.int32)[None, :]
    limit = jnp.sum(jnp.where(hits, counts[None, :], 0), axis=1)
    return jnp.clip(limit - ordinal * BLK, 0, BLK)


def block_slots(token_blocks, owner):
    adapters = owner.shape[0]
    key = owner * adapters + jnp.arange(adapters, dtype=jnp.int32)
    slot = jnp.sum((key[None, :] < key[:, None]).astype(jnp.int32), axis=1)
    hits = token_blocks[:, None] == jnp.arange(adapters, dtype=jnp.int32)[None, :]
    return jnp.sum(jnp.where(hits, slot[None, :], 0), axis=1)


def product_kernel(table, npieces, nrefs, has_acc, final, first, shares, info, *refs):
    sources = refs[:nrefs]
    rest = list(refs[nrefs:])
    w_ref = rest.pop(0)
    acc_in = rest.pop(0) if has_acc else None
    if final:
        s_ref, a0_ref, a1_ref, _ = rest[:4]
        rest = rest[4:]
    out_ref, weights, lhs, turned, acc, sems, weight_sems = rest
    f, c = pl.program_id(0), pl.program_id(1)
    last = npieces - 1
    ring, tile, width = weights.shape
    step = f * npieces + c
    steps = pl.num_programs(0) * npieces

    def weight_copy(t):
        k = first + lax.rem(t, npieces)
        column = jnp.where(info[1] == 0, k, shares - 1 - k) * width
        block = w_ref.at[
            pl.ds(pl.multiple_of(lax.div(t, npieces) * tile, tile), tile),
            pl.ds(pl.multiple_of(column, width), width),
        ]
        slot = lax.rem(t, ring)
        return pltpu.make_async_copy(block, weights.at[slot], weight_sems.at[slot])

    @pl.when(step == 0)
    def _():
        for i, places in enumerate(table):

            @pl.when(info[1] == i)
            def _():
                for k, (which, column) in enumerate(places):
                    source = sources[which].at[:, column : column + width]
                    pltpu.make_async_copy(source, lhs.at[k], sems.at[k]).start()

        for t in range(ring):
            weight_copy(t).start()

    @pl.when((step > 0) & (step + ring - 1 < steps))
    def _():
        weight_copy(step + ring - 1).start()

    for k in range(npieces):

        @pl.when((f == 0) & (c == k))
        def _():
            which, column = table[0][k]
            source = sources[which].at[:, column : column + width]
            pltpu.make_async_copy(source, lhs.at[k], sems.at[k]).wait()
            turned[k] = lhs[k].T

    weight_copy(step).wait()
    part = jnp.dot(
        weights[lax.rem(step, ring)], turned[c], preferred_element_type=jnp.float32
    )

    @pl.when(c == 0)
    def _():
        acc[...] = part + acc_in[...] if has_acc else part

    @pl.when(c > 0)
    def _():
        acc[...] += part

    @pl.when(c == last)
    def _():
        if final:
            finish_rows(
                acc, (s_ref[0], s_ref[1]), (a0_ref[0], a1_ref[0]), (info[4], info[5]), out_ref
            )
        else:
            out_ref[...] = acc[...]


def finish_rows(acc, terms, factors, lives, out_ref, turned=True):
    for b, factor in enumerate(factors):
        rows = slice(b * BLK, (b + 1) * BLK)
        extra = lax.dot_general(terms[b], factor, TN, preferred_element_type=jnp.float32)
        base = acc[:, rows].T if turned else acc[rows, :]
        live = lax.broadcasted_iota(jnp.int32, base.shape, 0) < lives[b]
        out_ref[rows, :] = jnp.where(live, base + extra, 0.0).astype(out_ref.dtype)


def shard_product(info, candidates, weight, first, npieces, shares, tile, acc_in=None, final=None, cost=LIGHT):
    width = weight.shape[1] // shares
    sources, table = [], []
    for i, pieces in enumerate(candidates):
        places = []
        for k in range(first, first + npieces):
            start = (k if i == 0 else shares - 1 - k) * width
            for begin, piece in pieces:
                if begin <= start < begin + piece.shape[1]:
                    known = [j for j, source in enumerate(sources) if source is piece]
                    if not known:
                        sources.append(piece)
                        known = [len(sources) - 1]
                    places.append((known[0], start - begin))
        table.append(places)
    share = sources[0].shape[0]
    units = weight.shape[0]

    anyspec = pl.BlockSpec(memory_space=pltpu.HBM)
    args = sources + [weight]
    specs = [anyspec] * (len(sources) + 1)
    if acc_in is not None:
        args.append(acc_in)
        specs.append(pl.BlockSpec((tile, share), lambda f, c, info: (f, 0)))
    aliases = {}
    if final is not None:
        scaled, factor, result = final
        rank = scaled.shape[1]
        aliases = {1 + len(args) + 3: 0}
        args += [scaled, factor, factor, result]
        specs += [
            pl.BlockSpec((SHARD_BLOCKS, rank, BLK), lambda f, c, info: (info[0], 0, 0)),
            pl.BlockSpec((1, rank, tile), lambda f, c, info: (info[2], 0, f)),
            pl.BlockSpec((1, rank, tile), lambda f, c, info: (info[3], 0, f)),
            anyspec,
        ]
        out_shape = jax.ShapeDtypeStruct(result.shape, result.dtype)
        out_spec = pl.BlockSpec((share, tile), lambda f, c, info: (info[0], f))
    else:
        out_shape = jax.ShapeDtypeStruct((units, share), jnp.float32)
        out_spec = pl.BlockSpec((tile, share), lambda f, c, info: (f, 0))
    return pl.pallas_call(
        functools.partial(
            product_kernel, table, npieces, len(sources), acc_in is not None, final is not None,
            first, shares,
        ),
        grid_spec=pltpu.PrefetchScalarGridSpec(
            num_scalar_prefetch=1,
            grid=(units // tile, npieces),
            in_specs=specs,
            out_specs=out_spec,
            scratch_shapes=[
                pltpu.VMEM((RING, tile, width), jnp.bfloat16),
                pltpu.VMEM((npieces, share, width), jnp.bfloat16),
                pltpu.VMEM((npieces, width, share), jnp.bfloat16),
                pltpu.VMEM((tile, share), jnp.float32),
                pltpu.SemaphoreType.DMA((npieces,)),
                pltpu.SemaphoreType.DMA((RING,)),
            ],
        ),
        out_shape=out_shape,
        input_output_aliases=aliases,
        compiler_params=pltpu.CompilerParams(
            dimension_semantics=("arbitrary", "arbitrary"), vmem_limit_bytes=VMEM_BYTES
        ),
        cost_estimate=cost,
        name="shard_product",
    )(info, *args)


RELAYS = (
    ((0, 1, 2), (3, 2, 1)),
    ((1, 2, 3), (2, 1, 0)),
    ((0, 2, 3), (3, 1, 0)),
)
TERMS = tuple(
    [(shard, me, -1) for shard in range(SHARES) if abs(shard - me) < 2]
    + [
        (shard, source, k)
        for k, moves in enumerate(RELAYS)
        for source, target, shard in moves
        if target == me
    ]
    for me in range(SHARES)
)


def low_kernel(table, nrefs, z_ref, adapters, *refs):
    sources = refs[:nrefs]
    factor, relays = refs[nrefs], refs[nrefs + 1 : nrefs + 1 + len(RELAYS)]
    out_ref, rows_ref, sems = refs[nrefs + 1 + len(RELAYS) :]
    width = rows_ref.shape[2]
    out_ref[...] = jnp.zeros_like(out_ref)
    for me, terms in enumerate(table):

        @pl.when(z_ref[0] == me)
        def _():
            copies = [
                pltpu.make_async_copy(
                    sources[which].at[:, column : column + width], rows_ref.at[i], sems.at[i]
                )
                for i, (_, _, which, column) in enumerate(terms)
            ]
            for copy in copies:
                copy.start()
            for i, (shard, relay, _, _) in enumerate(terms):
                copies[i].wait()
                for b in range(SHARD_BLOCKS):
                    block = shard * SHARD_BLOCKS + b
                    u = factor[adapters[block]] if relay < 0 else relays[relay][b]
                    rows = rows_ref[i, b * BLK : (b + 1) * BLK, :]
                    out_ref[block] += lax.dot_general(
                        rows, u, NT, preferred_element_type=jnp.float32
                    ).T


def low_terms(z, adapters, own, down, up, factor, relays):
    rank, width = factor.shape[1], factor.shape[2]
    sources = [own] + [piece for _, piece in down + up]
    table = []
    for me, terms in enumerate(TERMS):
        places = []
        for shard, part, relay in terms:
            pieces = [(0, own)] if shard == me else down if shard > me else up
            for begin, piece in pieces:
                if begin <= part * width < begin + piece.shape[1]:
                    which = [j for j, source in enumerate(sources) if source is piece][0]
                    places.append((shard, relay, which, part * width - begin))
        table.append(places)
    longest = max(len(places) for places in table)
    share = own.shape[0]
    vmem = pl.BlockSpec(memory_space=pltpu.VMEM)
    return pl.pallas_call(
        functools.partial(low_kernel, table, len(sources)),
        grid_spec=pltpu.PrefetchScalarGridSpec(
            num_scalar_prefetch=2,
            grid=(),
            in_specs=[pl.BlockSpec(memory_space=pltpu.HBM)] * len(sources)
            + [vmem] * (1 + len(relays)),
            out_specs=vmem,
            scratch_shapes=[
                pltpu.VMEM((longest, share, width), jnp.bfloat16),
                pltpu.SemaphoreType.DMA((longest,)),
            ],
        ),
        out_shape=jax.ShapeDtypeStruct((adapters.shape[0], rank, BLK), jnp.float32),
        compiler_params=pltpu.CompilerParams(vmem_limit_bytes=VMEM_BYTES),
        cost_estimate=LIGHT,
        name="low_terms",
    )(z, adapters, *sources, factor, *relays)


def adapter_kernel(n, table, nrefs, z_ref, slots, info, *refs):
    own, sources = refs[0], refs[1 : 1 + nrefs]
    s_in, s_out, x_ref, factor, acc0, acc1 = refs[1 + nrefs : 7 + nrefs]
    result_ref, down_ref, up_ref, rows_ref, sems = refs[7 + nrefs :]
    share = rows_ref.shape[0] // n
    width = rows_ref.shape[1]
    blocks = rows_ref.shape[0] // BLK
    z = z_ref[0]
    first = pl.program_id(0) == 0

    def each(do):
        for me, shard, which, column in table:

            @pl.when(z == me)
            def _():
                do(pltpu.make_async_copy(
                    sources[which].at[:, column : column + width],
                    rows_ref.at[shard * share : (shard + 1) * share, :],
                    sems.at[shard],
                ))

    def own_copy():
        return pltpu.make_async_copy(
            own.at[:, pl.ds(pl.multiple_of(z * width, width), width)],
            rows_ref.at[pl.ds(pl.multiple_of(z * share, share), share), :],
            sems.at[n],
        )

    @pl.when(first)
    def _():
        own_copy().start()
        each(lambda copy: copy.start())

    down_ref[...] = jnp.zeros_like(down_ref)
    for b in range(blocks):
        x = x_ref[b * BLK : (b + 1) * BLK, :]
        down_ref[slots[b]] += (1.0 / BLK) * jnp.dot(
            s_out[b], x, preferred_element_type=jnp.float32
        )
    for k, acc in enumerate((acc0, acc1)):
        rows = pl.ds(pl.multiple_of(info[k, 0] * share, share), share)
        terms = [s_out[info[k, 0] * SHARD_BLOCKS + b] for b in range(SHARD_BLOCKS)]
        factors = [factor[info[k, 2 + b]] for b in range(SHARD_BLOCKS)]
        lives = [info[k, 4 + b] for b in range(SHARD_BLOCKS)]
        finish_rows(acc, terms, factors, lives, result_ref.at[rows], turned=k == 1)

    @pl.when(first)
    def _():
        own_copy().wait()
        each(lambda copy: copy.wait())
        up_ref[...] = jnp.zeros_like(up_ref)
        for b in range(blocks):
            dy = rows_ref[b * BLK : (b + 1) * BLK, :]
            up_ref[slots[b]] += (1.0 / BLK) * jnp.dot(
                s_in[b], dy, preferred_element_type=jnp.float32
            )


def adapter_terms(z, slots, info, own, down, up, scaled_in, scaled_out, inputs, factor, acc0, acc1, n, tile):
    total, units = inputs.shape
    count_adapters, rank, _ = factor.shape
    share, width = own.shape[0], own.shape[1] // n
    sources, table = [], []
    for me in range(n):
        for shard in range(n):
            if shard == me:
                continue
            for begin, piece in down[shard - me] if shard > me else up[me - shard]:
                if begin <= me * width < begin + piece.shape[1]:
                    known = [j for j, source in enumerate(sources) if source is piece]
                    if not known:
                        sources.append(piece)
                        known = [len(sources) - 1]
                    table.append((me, shard, known[0], me * width - begin))
    anyspec = pl.BlockSpec(memory_space=pltpu.HBM)
    low_spec = pl.BlockSpec(scaled_in.shape, lambda f, *_: (0, 0, 0))
    factor_spec = pl.BlockSpec((count_adapters, rank, tile), lambda f, *_: (0, 0, f))
    return pl.pallas_call(
        functools.partial(adapter_kernel, n, table, len(sources)),
        grid_spec=pltpu.PrefetchScalarGridSpec(
            num_scalar_prefetch=3,
            grid=(units // tile,),
            in_specs=[anyspec] * (1 + len(sources))
            + [
                low_spec,
                low_spec,
                pl.BlockSpec((total, tile), lambda f, *_: (0, f)),
                factor_spec,
                pl.BlockSpec((share, tile), lambda f, *_: (0, f)),
                pl.BlockSpec((tile, share), lambda f, *_: (f, 0)),
            ],
            out_specs=[
                pl.BlockSpec((total, tile), lambda f, *_: (0, f)),
                factor_spec,
                pl.BlockSpec((count_adapters, rank, width), lambda f, *_: (0, 0, 0)),
            ],
            scratch_shapes=[
                pltpu.VMEM((total, width), jnp.bfloat16),
                pltpu.SemaphoreType.DMA((n + 1,)),
            ],
        ),
        out_shape=[
            jax.ShapeDtypeStruct((total, units), jnp.bfloat16),
            jax.ShapeDtypeStruct((count_adapters, rank, units), jnp.float32),
            jax.ShapeDtypeStruct((count_adapters, rank, width), jnp.float32),
        ],
        compiler_params=pltpu.CompilerParams(
            dimension_semantics=("arbitrary",), vmem_limit_bytes=VMEM_BYTES
        ),
        cost_estimate=LONG,
        name="adapter_terms",
    )(z, slots, info, own, *sources, scaled_in, scaled_out, inputs, factor, acc0, acc1)


def on_line(
    upstream,
    hidden,
    frozen_weight,
    adapter_down_factor,
    adapter_up_factor,
    live_row_counts,
    adapter_of_block,
    gradient_owner_group,
):
    n = SHARES
    z = lax.axis_index("tp")
    own = upstream[0]
    share, features = own.shape
    width = features // n
    total = share * n
    units = hidden.shape[2]
    adapters = gradient_owner_group.shape[0]

    token_blocks = adapter_of_block[0]
    counts = live_counts(token_blocks, live_row_counts[0])
    slots = block_slots(token_blocks, gradient_owner_group)
    live = jnp.arange(BLK, dtype=jnp.int32)[None, None, :] < counts[:, None, None]
    inputs = hidden[0]

    def info_of(shard, candidate):
        pair = shard * SHARD_BLOCKS + jnp.arange(SHARD_BLOCKS, dtype=jnp.int32)
        hits = pair[:, None] == jnp.arange(token_blocks.shape[0], dtype=jnp.int32)[None, :]
        names = jnp.sum(jnp.where(hits, token_blocks[None, :], 0), axis=1)
        lives = jnp.sum(jnp.where(hits, counts[None, :], 0), axis=1)
        head = jnp.stack([shard, candidate]).astype(jnp.int32)
        return jnp.concatenate([head, names, lives])

    lower = (z >= n // 2).astype(jnp.int32)
    top = (z == n - 1).astype(jnp.int32)
    infos = [
        info_of(z, jnp.zeros((), jnp.int32)),
        info_of(jnp.where(top == 1, z - 1, z + 1), top),
        info_of(jnp.where(lower == 1, z - 2, z + 2), lower),
        info_of(
            jnp.where(z == 0, n - 1, jnp.where(top == 1, 0, z - 1)), jnp.minimum(z, 1) + top
        ),
    ]

    def held(value, *after):
        return lax.optimization_barrier((value, after))[0] if after else value

    def pair_sum(terms, distance, *after):
        pairs = [(s, s ^ distance) for s in range(n)]
        return held(terms + lax.ppermute(terms, "tp", pairs), *after)

    one_down = [(s, s - 1) for s in range(1, n)]
    one_up = [(s, s + 1) for s in range(n - 1)]
    two_down = [(s, s - 1) for s in range(1, n - 1)]
    two_up = [(s, s + 1) for s in range(1, n - 1)]
    far_down, far_up = [(n - 1, 0)], [(0, n - 1)]

    def move(pieces, pairs, *after):
        return [(begin, lax.ppermute(held(piece, *after), "tp", pairs)) for begin, piece in pieces]

    tile = 1024
    half = features // 2
    low, high = own[:, :half], own[:, half:]
    near_d = move([(0, low), (half, high)], one_down)
    near_u = move([(0, low), (half, high)], one_up)
    up_factor_block = adapter_up_factor[token_blocks]

    def relay(moves):
        shard = sum(jnp.where(z == source, goes, 0) for source, _, goes in moves)
        part = lax.dynamic_slice_in_dim(up_factor_block, shard * SHARD_BLOCKS, SHARD_BLOCKS, 0)
        return lax.ppermute(part, "tp", [(source, target) for source, target, _ in moves])

    relays = [relay(moves) for moves in RELAYS]
    part_in = jnp.einsum(
        "bif,brf->bri",
        inputs.reshape(-1, BLK, units),
        adapter_down_factor[token_blocks],
        preferred_element_type=jnp.float32,
    )
    rest = held(own, part_in)
    first, middle, last = rest[:, :width], rest[:, width:-width], rest[:, -width:]
    corner = near_d[0][1][:8, :BLK]
    acc_own = lax.dot_general(
        held(own, corner), frozen_weight, NT, preferred_element_type=jnp.float32
    )
    place = z.reshape(1).astype(jnp.int32)
    phase = (near_d[1], near_u[1], acc_own)
    two_d = move(near_d[:1], two_down, phase)
    two_u = move(near_u[1:], two_up, phase)
    part_out = low_terms(
        place, held(token_blocks, phase), own, near_d, near_u, adapter_up_factor, relays
    )
    acc_one = shard_product(
        held(infos[1], part_out), [near_d, near_u], frozen_weight, 0, n, n, tile, cost=LONG
    )
    low = pair_sum(held(jnp.stack([part_in, part_out]), acc_one), 1)
    far_d = move([(0, first)], far_down, low)
    far_u = move([(features - width, last)], far_up, low)
    low = pair_sum(held(low, two_d[0], two_u[0]), 2)
    scaled = jnp.where(live[None], adapter_scale * low, 0.0).astype(jnp.bfloat16)
    scaled_in, scaled_out = scaled[0], scaled[1]
    two_d += move(near_d[1:], two_down, low)
    two_u += move(near_u[:1], two_up, low)
    result, slot_down, slot_up = adapter_terms(
        place, slots, jnp.stack(infos[:2]), own,
        {1: near_d, 2: two_d[:1], 3: far_d[:1]}, {1: near_u, 2: two_u[:1], 3: far_u[:1]},
        scaled_in, scaled_out, inputs, adapter_down_factor, acc_own, acc_one, n, tile,
    )
    grad_up = lax.psum_scatter(slot_up, "dp", scatter_dimension=0, tiled=True)
    grad_down = lax.psum_scatter(slot_down, "dp", scatter_dimension=0, tiled=True)
    phase = (two_d[1], two_u[1], result)
    far_d += move([(width, middle), (features - width, last)], far_down, phase)
    far_u += move([(width, middle), (0, first)], far_up, phase)
    result = shard_product(
        held(infos[2], phase), [two_d, two_u], frozen_weight, 0, n, n,
        tile, final=(scaled_out, adapter_down_factor, result), cost=LONG,
    )
    acc_last = shard_product(
        held(infos[3], result), [far_d[:2], near_u, far_u[:2]], frozen_weight, 0, n - 1, n, tile
    )
    result = shard_product(
        infos[3], [far_d[2:], near_u, far_u[2:]], frozen_weight, n - 1, 1, n, tile,
        acc_in=acc_last, final=(scaled_out, adapter_down_factor, result),
    )
    return (result[None], grad_down, grad_up)


def gathered(
    upstream,
    hidden,
    frozen_weight,
    adapter_down_factor,
    adapter_up_factor,
    live_row_counts,
    adapter_of_block,
    gradient_owner_group,
):
    token_blocks = adapter_of_block[0]
    counts = live_counts(token_blocks, live_row_counts[0])
    slots = block_slots(token_blocks, gradient_owner_group)
    live = jnp.arange(BLK, dtype=jnp.int32)[None, :, None] < counts[:, None, None]
    inputs = hidden[0].reshape(-1, BLK, hidden.shape[2])
    down_factor = adapter_down_factor[token_blocks]
    local = adapter_up_factor.shape[2]
    grad_rows = lax.all_gather(upstream[0], "tp", axis=0, tiled=True)
    grad_slice = lax.dynamic_slice_in_dim(grad_rows, lax.axis_index("tp") * local, local, 1)
    grad_blk = grad_slice.reshape(-1, BLK, local)
    dot = functools.partial(jnp.einsum, preferred_element_type=jnp.float32)
    low_in, low_out = lax.psum(
        (
            dot("bif,brf->bir", inputs, down_factor),
            dot("bik,brk->bir", grad_blk, adapter_up_factor[token_blocks]),
        ),
        "tp",
    )
    scaled_in = jnp.where(live, adapter_scale * low_in, 0.0).astype(jnp.bfloat16)
    scaled_out = jnp.where(live, adapter_scale * low_out, 0.0).astype(jnp.bfloat16)
    base = lax.dot_general(grad_rows, frozen_weight, NT, preferred_element_type=jnp.float32)
    extra = dot("bir,brf->bif", scaled_out, down_factor)
    result = jnp.where(live, base.reshape(extra.shape) + extra, 0.0).astype(jnp.bfloat16)
    names = jnp.arange(gradient_owner_group.shape[0], dtype=jnp.int32)
    select = (names[:, None] == slots[None, :]).astype(jnp.float32)
    exact = functools.partial(jnp.einsum, precision=lax.Precision.HIGHEST)
    slot_down = exact("sb,brf->srf", select, dot("bir,bif->brf", scaled_out, inputs))
    slot_up = exact("sb,brk->srk", select, dot("bir,bik->brk", scaled_in, grad_blk))
    owned_down = lax.psum_scatter(slot_down, "dp", scatter_dimension=0, tiled=True)
    owned_up = lax.psum_scatter(slot_up, "dp", scatter_dimension=0, tiled=True)
    result = result.reshape(1, grad_rows.shape[0], -1)
    return (result, owned_down * (1.0 / BLK), owned_up * (1.0 / BLK))


def solution(mesh):
    return jax.shard_map(
        on_line if mesh.shape["tp"] == SHARES else gathered,
        mesh=mesh,
        in_specs=(
            P(("rep", "dp"), "tp", None),
            P(("rep", "dp"), None, "tp"),
            P("tp", None),
            P("rep", None, "tp"),
            P("rep", None, "tp"),
            P(("rep", "dp"), None),
            P(("rep", "dp"), None),
            P("rep"),
        ),
        out_specs=(
            P(("rep", "dp"), None, "tp"),
            P(("rep", "dp"), None, "tp"),
            P(("rep", "dp"), None, "tp"),
        ),
        check_vma=False,
    )
```
